512 devices in a mesh: tp: 8 (over y), fsdp: 64 (over z, x, core).
Axes of the slice: x: 4, y: 8, z: 8, core: 2. Of those that a mesh axis runs over, the one named last changes fastest.
Arguments:
- decoded: bfloat16 [8192, 4096], P('fsdp', 'tp'), may hold values from -6 to 6
- lengths: int32 [64, 8], P('fsdp'), may hold values from 1 to 32, 128 in all within a row
- destination: int32 [8192, 1], P('fsdp'), may hold values from 0 to 63; in each aligned block of 128 rows (0 to 127, 128 to 255, ...) at most 2 rows name the same one
- attn_gain: bfloat16 [4096], replicated, may hold values from 0.099609375 to 1.8984375
- query_weight: bfloat16 [4096, 4096], P('fsdp', 'tp'), may hold values from -1.5625 to 1.5625, as said below
- key_weight: bfloat16 [4096, 256], P('fsdp'), may hold values from -0.0625 to 0.0625, as said below
- value_weight: bfloat16 [4096, 256], P('fsdp'), may hold values from -0.09375 to 0.09375
- out_weight: bfloat16 [4096, 4096], P('tp', 'fsdp'), may hold values from -0.09375 to 0.09375
- final_gain: bfloat16 [4096], P('tp'), may hold values from 0.099609375 to 1.8984375
- head_weight: bfloat16 [4096], P('tp'), may hold values from -0.09375 to 0.09375
Outputs:
- hidden: bfloat16 [8192, 4096], P('fsdp', 'tp')
- rewards: float32 [512], P('fsdp')
The draws below stay inside these ranges and needn't reach their ends.
Inputs may be any that keep to these rules, and one draw needn't show every extreme that they name: `destination`: in each decode group's 128 rows every reward shard is named by exactly 2 rows. Each decode group's 8 lengths add up to 128; in each group the longest is 32. `query_weight`: entries of order one over the square root of 4096. `key_weight`: entries of order one over the square root of 4096.
All inputs are finite; a program needn't handle non-finite values.
Results may differ from the reference program's by a relative error of at most 0.017.
Values may be sent and summed in bfloat16 or wider, within the bound.
No kernel may reach another device: no remote copies, remote signals or barrier semaphores. Data moves between devices by JAX's collectives and lax.ppermute only.
A program may use at most 64 MiB of HBM per device.

```python
import math
import jax
import jax.numpy as jnp
import numpy as np
from jax import lax

D = 4096
HD = 128
QH = 32
KVH = 2
ROWS = 128
RESP_DEV = 8
LMAX = 32
CAP = 2
TOKENS = 8192
RESP = 512
N_TP = 8
N_FSDP = 64


def shared_base(key):
    return jax.random.truncated_normal(key, -4.0, 4.0, (D, KVH * HD), jnp.float32)


def draw_key_weight(key, part):
    shared = shared_base(key)
    return (shared * D ** (-0.5)).astype(jnp.bfloat16)


def draw_query_weight(key, part):
    key = jax.random.fold_in(key, 5)
    noise_key = jax.random.fold_in(key, 0)
    noise_part = jax.random.truncated_normal(noise_key, -4.0, 4.0, (D, QH * HD), jnp.float32)
    return (noise_part * D ** (-0.5)).astype(jnp.bfloat16)


def block_scale(own_key, shape, cuts, low, high):
    gain = 1.0
    for axis_at, parts in cuts:
        draws = jax.random.uniform(jax.random.fold_in(jax.random.fold_in(own_key, 6), axis_at), (parts,), jnp.float32, low / len(cuts), high / len(cuts))
        gain = gain * jnp.repeat(jnp.exp(draws), shape[axis_at] // parts).reshape((-1,) + (1,) * (len(shape) - 1 - axis_at))
    return gain


def profile(amount, total, bound, slope):
    loads = [(1 << 20) // math.isqrt(rank ** slope) + 1 for rank in range(2, amount + 1)]
    spare, holding = total - bound - (amount - 1), [1] * (amount - 1)
    while spare > 0:
        movable = [i for i in range(amount - 1) if holding[i] < bound]
        mass, left = sum([loads[i] for i in movable]), spare
        for i in movable:
            addition = min(bound - holding[i], max(1, left * loads[i] // mass), spare)
            holding[i] = holding[i] + addition
            spare = spare - addition
    return np.array([bound] + holding)


def ragged_sizes(stream_key, amount, total, reach, skew):
    if amount == 2:
        one = jax.random.randint(stream_key, (), max(1, total - reach), min(reach, total - 1) + 1)
        return jnp.stack([one, total - one])
    sizes = jnp.asarray(profile(amount, total, reach, skew), jnp.int32)
    twos = (amount - 1) // 2
    source_of, receiver = sizes[1:1 + 2 * twos:2], sizes[2:2 + 2 * twos:2]
    slack = jnp.minimum(source_of - 1, reach - receiver)
    moved = jax.random.randint(jax.random.fold_in(stream_key, 1), (twos,), 0, 1 << 20) % (slack + 1)
    sizes = sizes.at[1:1 + 2 * twos:2].set(source_of - moved).at[2:2 + 2 * twos:2].set(receiver + moved)
    return sizes[jax.random.permutation(jax.random.fold_in(stream_key, 2), amount)]


def shared_out(rng, own, number, rows, count, top, most, slope):
    order = jax.random.permutation(rng, count)
    crowded, usual = portions_of(count, rows * top, most, slope, True), portions_of(count, rows * top, most, slope, False)
    places = jnp.arange(count)

    def named(sizes, offset_by):
        used = int((sizes > 0).sum())
        fixed = max(1, used // 4)
        passed = fixed + (places - fixed + offset_by * (used - fixed)) % max(1, count - fixed)
        return jnp.zeros((count,), jnp.int32).at[order[jnp.where(places < fixed, places, passed)]].set(jnp.asarray(sizes, jnp.int32))

    sizes = jnp.where(number % 4 == 0, named(crowded, number // 4), named(usual, number - number // 4 - 1))
    mixed = jax.random.permutation(jax.random.fold_in(own, 3), count)
    giver, receiver = mixed[0:count // 2 * 2:2], mixed[1:count // 2 * 2:2]
    slack = jnp.minimum(sizes[giver] - 1, most - sizes[receiver]) // 2
    slack = jnp.where((giver == order[0]) | (receiver == order[0]) | (sizes[receiver] == 0), 0, jnp.maximum(slack, 0))
    passed = jax.random.randint(jax.random.fold_in(own, 4), (count // 2,), 0, 1 << 20) % (slack + 1)
    sizes = sizes.at[giver].add(-passed).at[receiver].add(passed)
    members = jnp.searchsorted(jnp.cumsum(sizes), jnp.arange(rows * top), side="right").astype(jnp.int32)
    table = members.reshape(top, rows).T
    table = table[jax.random.permutation(jax.random.fold_in(own, 1), rows)]
    offset_by = jax.random.randint(jax.random.fold_in(own, 2), (rows, 1), 0, top)
    return jnp.take_along_axis(table, (jnp.arange(top)[None, :] + offset_by) % top, axis=1)


def portions_of(count, total, reach, slope, full):
    portions = [(1 << 20) // math.isqrt(standing ** slope) + 1 for standing in range(1, count + 1)]
    largest = reach if full else min(reach, max(-(-total // count), total * portions[0] // sum(portions)))
    least = 1 if total - largest >= count - 1 else 0
    holding, rest = [largest] + [least] * (count - 1), total - largest - least * (count - 1)
    while rest > 0:
        candidates = [i for i in range(1, count) if holding[i] < largest] or [i for i in range(1, count) if holding[i] < reach]
        pool, budget = sum([portions[i] for i in candidates]), rest
        for i in candidates:
            more = min(reach - holding[i], max(1, budget * portions[i] // pool), rest)
            holding[i] = holding[i] + more
            rest = rest - more
    return np.array(holding)


def gaussian(rng, shape, spread, reach, shards=(), held_as=jnp.bfloat16):
    values = jax.random.normal(rng, shape, jnp.float32) * spread
    if len(shards) > 0:
        values = block_scale(rng, shape, shards, -0.22, 0.18) * values
    return jnp.clip(values, min=-reach, max=reach).astype(held_as)


def setup_inputs(seed: int = 0) -> dict:
    key_of = jax.random.split(jax.random.key(seed), 11)
    decoded = gaussian(key_of[0], (TOKENS, D), 1.0, 6.0, ((0, 64), (1, 8)))
    lengths = jax.vmap(lambda own: ragged_sizes(own, RESP_DEV, ROWS, LMAX, 2))(jax.random.split(key_of[1], N_FSDP)).reshape((N_FSDP, RESP_DEV)).astype(jnp.int32)
    destination_keys = jax.random.split(jax.random.fold_in(key_of[2], 1), TOKENS // ROWS)
    destination_turns = jax.random.permutation(jax.random.fold_in(key_of[2], 3), TOKENS // ROWS)
    destination = jax.vmap(lambda own, number: shared_out(jax.random.fold_in(key_of[2], 2), own, number, ROWS, N_FSDP, 1, CAP, 0))(destination_keys, destination_turns).reshape((TOKENS, 1))
    attn_gain = jnp.clip(1.0 + 0.18 * jax.random.normal(key_of[3], (D,), jnp.float32), 0.099609375, 1.8984375).astype(jnp.bfloat16)
    query_weight = draw_query_weight(jax.random.fold_in(key_of[10], 71), 0)
    key_weight = draw_key_weight(jax.random.fold_in(key_of[10], 71), 0)
    value_weight = gaussian(key_of[6], (D, KVH * HD), D ** -0.5, 0.09375, ((0, 64),))
    out_weight = gaussian(key_of[7], (QH * HD, D), (QH * HD) ** -0.5, 0.09375, ((0, 8), (1, 64)))
    final_gain = jnp.clip(1.0 + 0.18 * jax.random.normal(key_of[8], (D,), jnp.float32), 0.099609375, 1.8984375).astype(jnp.bfloat16)
    head_weight = gaussian(key_of[9], (D,), D ** -0.5, 0.09375, ((0, 8),))
    return dict(decoded=decoded, lengths=lengths, destination=destination, attn_gain=attn_gain, query_weight=query_weight, key_weight=key_weight, value_weight=value_weight, out_weight=out_weight, final_gain=final_gain, head_weight=head_weight)


norm_eps = 1e-06
rope_base = 1000000.0
neg_fill = -1e+30

def rotate(heads_in, positions):
    half_size = heads_in.shape[-1] // 2
    frequency = rope_base ** (-(jnp.arange(half_size, dtype=jnp.float32) * 2.0 / heads_in.shape[-1]))
    angles = positions.astype(jnp.float32)[:, None] * frequency[None, :]
    cosine = jnp.cos(angles)[:, None, :]
    sine_part = jnp.sin(angles)[:, None, :]
    front_half = heads_in[..., :half_size]
    back_half = heads_in[..., half_size:]
    return jnp.concatenate([front_half * cosine - back_half * sine_part, back_half * cosine + front_half * sine_part], axis=-1)

def rounded(values_in):
    return lax.optimization_barrier(values_in.astype(jnp.bfloat16)).astype(jnp.float32)

def reference(decoded, lengths, destination, attn_gain, query_weight, key_weight, value_weight, out_weight, final_gain, head_weight):
    row_index = jnp.arange(ROWS, dtype=jnp.int32)
    resp_ends = jnp.cumsum(lengths, axis=1).astype(jnp.int32)
    resp_local = lax.optimization_barrier(jnp.sum((row_index[None, :, None] >= resp_ends[:, None, :]).astype(jnp.int32), axis=2)).astype(jnp.int32)
    resp_length = jnp.take_along_axis(lengths, resp_local, axis=1)
    resp_stop = jnp.take_along_axis(resp_ends, resp_local, axis=1)
    positions = row_index[None, :] - (resp_stop - resp_length)
    is_last = positions == resp_length - 1
    grouped = decoded.reshape(N_FSDP, ROWS, D)
    head_width = QH * HD // N_TP

    def one_group(packed):
        block_rows, local_ids, local_pos, local_last = packed
        widened = block_rows.astype(jnp.float32)
        normed = (widened * lax.rsqrt(lax.optimization_barrier(jnp.mean(widened * widened, axis=1, keepdims=True)) + norm_eps) * attn_gain.astype(jnp.float32)).astype(jnp.bfloat16)
        queries = jnp.dot(normed, query_weight, preferred_element_type=jnp.float32).reshape(ROWS, QH, HD)
        key_heads = jnp.dot(normed, key_weight, preferred_element_type=jnp.float32).reshape(ROWS, KVH, HD)
        value_heads = rounded(jnp.dot(normed, value_weight, preferred_element_type=jnp.float32).reshape(ROWS, KVH, HD))
        queries = rounded(rotate(queries, local_pos))
        key_heads = rounded(rotate(key_heads, local_pos))
        key_heads = jnp.repeat(key_heads, QH // KVH, axis=1)
        value_heads = jnp.repeat(value_heads, QH // KVH, axis=1)
        scores = jnp.einsum('shd,khd->hsk', queries, key_heads) / math.sqrt(HD)
        allowed = (local_ids[:, None] == local_ids[None, :]) & (local_pos[None, :] <= local_pos[:, None])
        scores = jnp.where(allowed[None], scores, neg_fill)
        row_max = lax.optimization_barrier(jnp.max(scores, axis=2, keepdims=True))
        weights = jnp.where(allowed[None], jnp.exp(scores - row_max), 0.0)
        totals = lax.optimization_barrier(jnp.sum(weights, axis=2))
        attended = jnp.einsum('hsk,khd->shd', rounded(weights), value_heads) / jnp.transpose(totals)[:, :, None]
        attended = attended.reshape(ROWS, QH * HD).astype(jnp.bfloat16)
        update = jnp.zeros((ROWS, D), jnp.float32)
        for tp_part in range(N_TP):
            columns = attended[:, tp_part * head_width:(tp_part + 1) * head_width]
            weight_rows = out_weight[tp_part * head_width:(tp_part + 1) * head_width]
            update = update + rounded(jnp.dot(columns, weight_rows, preferred_element_type=jnp.float32))
        layer_rows = (widened + update).astype(jnp.bfloat16)
        layer_wide = layer_rows.astype(jnp.float32)
        product = lax.optimization_barrier(jnp.sum(layer_wide * final_gain.astype(jnp.float32) * head_weight.astype(jnp.float32), axis=1))
        row_reward = lax.rsqrt(lax.optimization_barrier(jnp.mean(layer_wide * layer_wide, axis=1)) + norm_eps) * product
        picked = ((local_ids[:, None] == jnp.arange(RESP_DEV, dtype=jnp.int32)[None, :]) & local_last[:, None]).astype(jnp.float32)
        return (layer_rows, lax.optimization_barrier(jnp.sum(picked * row_reward[:, None], axis=0)))
    layer_all, rewards = lax.map(one_group, (grouped, resp_local, positions, is_last))
    dest_shard = destination[:, 0].reshape(N_FSDP, ROWS)
    dest_hits = (dest_shard[:, :, None] == jnp.arange(N_FSDP, dtype=jnp.int32)[None, None, :]).astype(jnp.int32)
    dest_rank = lax.optimization_barrier(jnp.sum(jnp.cumsum(dest_hits, axis=1) * dest_hits, axis=2)) - 1
    source_index = jnp.arange(N_FSDP, dtype=jnp.int32)[:, None]
    placed = (dest_shard * ROWS + source_index * (ROWS // N_FSDP) + dest_rank).astype(jnp.int32)
    hidden = jnp.zeros((TOKENS, D), jnp.bfloat16).at[placed.reshape(TOKENS)].set(layer_all.reshape(TOKENS, D))
    return (hidden, rewards.reshape(RESP))
```

```python
import jax
import jax.numpy as jnp
from jax import lax
from jax.experimental import pallas as pl
from jax.experimental.pallas import tpu as pltpu
from jax.sharding import Mesh, PartitionSpec as P

D = 4096
HD = 128
QH = 32
KVH = 2
NT, NZ, NX, NC = 8, 8, 4, 2
ROWS = 128
FEAT = D // NT
BLK = 128
QW = QH * HD // NT
PW = QW + 2 * HD
HEADS = QW // HD
EXTRA = 16
RESP = 8

norm_eps = 1e-06
rope_base = 1000000.0
neg_fill = -1e30

bf16 = jnp.bfloat16
f32 = jnp.float32

VMEM = pl.BlockSpec(memory_space=pltpu.VMEM)
SMEM = pl.BlockSpec(memory_space=pltpu.SMEM)


def call(kernel, out_shape, in_specs, scratch=(), flops=0, name=None):
    return pl.pallas_call(
        kernel,
        out_shape=out_shape,
        in_specs=in_specs,
        out_specs=jax.tree.map(lambda _: VMEM, out_shape),
        scratch_shapes=list(scratch),
        compiler_params=pltpu.CompilerParams(vmem_limit_bytes=24 * 1024 * 1024),
        cost_estimate=pl.CostEstimate(flops=flops, bytes_accessed=4 << 20, transcendentals=0),
        name=name,
    )


def iota(shape, axis):
    return lax.broadcasted_iota(jnp.int32, shape, axis)


def eye_mask():
    return iota((ROWS, ROWS), 0) == iota((ROWS, ROWS), 1)


def resp_starts(lengths_ref, rows):
    end = jnp.int32(0)
    start = jnp.zeros_like(rows)
    for j in range(RESP):
        end = end + lengths_ref[0, j]
        start = jnp.where(rows >= end, end, start)
    return start


def project_kernel(core_ref, x_ref, own_ref, other_ref, gain_ref, out_ref, xs_ref, w_ref):
    first = core_ref[0] == 0
    for t in range(NT):
        own, other = own_ref[t], other_ref[t]
        w_ref[t * BLK : t * BLK + BLK // 2, :] = jnp.where(first, own, other)
        w_ref[t * BLK + BLK // 2 : (t + 1) * BLK, :] = jnp.where(first, other, own)
    eye = eye_mask()
    for g in range(NX):
        square = jnp.zeros((ROWS, BLK), f32)
        for t in range(NT):
            wide = x_ref[t * NX + g].astype(f32)
            square = square + wide * wide
            xs_ref[g * ROWS : (g + 1) * ROWS, t * BLK : (t + 1) * BLK] = (
                wide * gain_ref[t : t + 1, :].astype(f32)
            ).astype(bf16)
        total = jnp.sum(square, axis=1, keepdims=True)
        line = jnp.sum(jnp.where(eye, total, 0.0), axis=0, keepdims=True)
        high = line.astype(bf16).astype(f32)
        low = line - high
        which = iota((EXTRA, ROWS), 0)
        tail = jnp.where(which == 0, high, jnp.where(which == 1, low, 0.0)).astype(bf16)
        out_ref[g, ROWS:, :] = jnp.concatenate(
            [tail, jnp.zeros((EXTRA, PW - ROWS), bf16)], axis=1
        )
    for n in range(PW // 256):
        cols = slice(n * 256, (n + 1) * 256)
        part = jnp.dot(xs_ref[...], w_ref[:, cols], preferred_element_type=f32)
        for g in range(NX):
            out_ref[g, :ROWS, cols] = part[g * ROWS : (g + 1) * ROWS].astype(bf16)


def attend_kernel(lengths_ref, parts_ref, freq_ref, out_ref):
    eye = eye_mask()
    line = jnp.zeros((EXTRA, ROWS), f32)
    for i in range(NX):
        line = line + parts_ref[i, ROWS:, :ROWS].astype(f32)
    line = jnp.sum(line, axis=0, keepdims=True)
    total = jnp.sum(jnp.where(eye, line, 0.0), axis=1, keepdims=True)
    scale = lax.rsqrt(total * (1.0 / D) + norm_eps)

    rows = iota((ROWS, ROWS), 0)
    cols = iota((ROWS, ROWS), 1)
    start = resp_starts(lengths_ref, rows)
    allowed = (cols >= start) & (cols <= rows)
    angles = (rows - start).astype(f32) * freq_ref[...]
    cosine = jnp.cos(angles)
    sine = jnp.sin(angles)
    sine = jnp.where(cols < HD // 2, -sine, sine)

    def columns(at):
        summed = parts_ref[0, :ROWS, at : at + HD].astype(f32)
        for i in range(1, NX):
            summed = summed + parts_ref[i, :ROWS, at : at + HD].astype(f32)
        return summed * scale

    def rope(v):
        return (v * cosine + pltpu.roll(v, HD // 2, 1) * sine).astype(bf16)

    keys = rope(columns(QW))
    values = columns(QW + HD).astype(bf16)
    for h in range(HEADS):
        queries = rope(columns(h * HD))
        scores = lax.dot_general(
            queries, keys, (((1,), (1,)), ((), ())), preferred_element_type=f32
        ) * (HD**-0.5)
        scores = jnp.where(allowed, scores, neg_fill)
        top = jnp.max(scores, axis=1, keepdims=True)
        probs = jnp.where(allowed, jnp.exp(scores - top), 0.0)
        sums = jnp.sum(probs, axis=1, keepdims=True)
        weighted = jnp.dot(probs.astype(bf16), values, preferred_element_type=f32)
        out_ref[:, h * HD : (h + 1) * HD] = (weighted / sums).astype(bf16)


def output_kernel(x_ref, w_ref, out_ref):
    for n in range(NT // 2):
        part = lax.dot_general(
            x_ref[...],
            w_ref[n * 2 * BLK : (n + 1) * 2 * BLK, :],
            (((1,), (1,)), ((), ())),
            preferred_element_type=f32,
        )
        for g in range(NX):
            rows = part[g * ROWS : (g + 1) * ROWS].astype(bf16)
            out_ref[2 * n * NX + g] = rows[:, :BLK]
            out_ref[(2 * n + 1) * NX + g] = rows[:, BLK:]


def layer_kernel(lengths_ref, parts_ref, rows_ref, line_ref, final_ref, head_ref, out_ref, stat_ref):
    dest_line = line_ref[...]
    eye = eye_mask()
    dest_column = jnp.sum(jnp.where(eye, dest_line, 0), axis=1, keepdims=True)
    same = (dest_column == dest_line) & (iota((ROWS, ROWS), 0) < iota((ROWS, ROWS), 1))
    rank = jnp.sum(same.astype(jnp.int32), axis=0, keepdims=True)
    slot = dest_line * (ROWS // (NZ * NX * NC)) + rank
    order = (iota((ROWS, ROWS), 0) == slot).astype(f32).astype(bf16)

    square = jnp.zeros((ROWS, BLK), f32)
    product = jnp.zeros((ROWS, BLK), f32)
    for g in range(NX):
        cols = slice(g * BLK, (g + 1) * BLK)
        update = parts_ref[g].astype(f32)
        for t in range(1, NT):
            update = update + parts_ref[t * NX + g].astype(f32)
        layer = (rows_ref[:, cols].astype(f32) + update).astype(bf16)
        wide = layer.astype(f32)
        square = square + wide * wide
        product = product + wide * final_ref[:, cols].astype(f32) * head_ref[:, cols].astype(f32)
        out_ref[:, cols] = jnp.dot(order, layer, preferred_element_type=f32).astype(bf16)

    lane = iota((1, BLK), 1)
    last = jnp.full((1, BLK), -1, jnp.int32)
    end = jnp.int32(0)
    for j in range(RESP):
        end = end + lengths_ref[0, j]
        last = jnp.where(lane == j, end - 1, last)
    pick = iota((ROWS, BLK), 0) == last
    for at, part in ((0, square), (1, product)):
        column = jnp.sum(part, axis=1, keepdims=True)
        stat_ref[at : at + 1, :] = jnp.sum(jnp.where(pick, column, 0.0), axis=0, keepdims=True)


def body(
    decoded,
    lengths,
    destination,
    attn_gain,
    query_weight,
    key_weight,
    value_weight,
    out_weight,
    final_gain,
    head_weight,
):
    me_t, me_x, me_c = lax.axis_index("tp"), lax.axis_index("x"), lax.axis_index("core")
    fsdp = ("z", "x", "core")

    mine = out_weight.T
    theirs = lax.ppermute(mine, "core", [(0, 1), (1, 0)])
    both = jnp.where(
        me_c == 0, jnp.concatenate([mine, theirs]), jnp.concatenate([theirs, mine])
    )
    out_rows = lax.all_gather(both, "z", axis=0, tiled=True)

    sent = jnp.broadcast_to(
        decoded.reshape(ROWS, NX, BLK).transpose(1, 0, 2)[None], (NT, NX, ROWS, BLK)
    ).reshape(NT * NX, ROWS, BLK)
    tokens = lax.all_to_all(sent, ("tp", "x"), split_axis=0, concat_axis=0, tiled=True)

    kv_at = me_t // (NT // KVH) * HD
    shard = jnp.concatenate(
        [
            query_weight,
            lax.dynamic_slice_in_dim(key_weight, kv_at, HD, 1),
            lax.dynamic_slice_in_dim(value_weight, kv_at, HD, 1),
        ],
        axis=1,
    )
    own = lax.all_gather(shard, "z", axis=0, tiled=False)
    other = lax.ppermute(own, "core", [(0, 1), (1, 0)])
    gain = lax.dynamic_slice_in_dim(attn_gain.reshape(NT, NX, BLK), me_x, 1, 1)[:, 0]

    partial_sums = call(
        project_kernel,
        jax.ShapeDtypeStruct((NX, ROWS + EXTRA, PW), bf16),
        [SMEM, VMEM, VMEM, VMEM, VMEM],
        [pltpu.VMEM((NX * ROWS, NT * BLK), bf16), pltpu.VMEM((NT * BLK, PW), bf16)],
        flops=2 * 512 * 1024 * 768,
        name="project",
    )(me_c.reshape(1).astype(jnp.int32), tokens, own, other, gain)
    summands = lax.all_to_all(partial_sums, "x", split_axis=0, concat_axis=0, tiled=True)

    half = jnp.arange(HD // 2, dtype=f32)
    freq = rope_base ** (-(half * 2.0 / HD))
    freq = jnp.concatenate([freq, freq])[None]
    attended = call(
        attend_kernel,
        jax.ShapeDtypeStruct((ROWS, QW), bf16),
        [SMEM, VMEM, VMEM],
        flops=2 * 128 * 128 * 128 * 8,
        name="attend",
    )(lengths, summands, freq)

    slab = lax.all_gather(attended, "x", axis=0, tiled=True)
    products = call(
        output_kernel,
        jax.ShapeDtypeStruct((NT * NX, ROWS, BLK), bf16),
        [VMEM, VMEM],
        flops=2 * 512 * 512 * 1024,
        name="output",
    )(slab, out_rows)
    terms = lax.all_to_all(products, ("tp", "x"), split_axis=0, concat_axis=0, tiled=True)

    placed, stat = call(
        layer_kernel,
        (jax.ShapeDtypeStruct((ROWS, FEAT), bf16), jax.ShapeDtypeStruct((2, BLK), f32)),
        [SMEM, VMEM, VMEM, VMEM, VMEM, VMEM],
        flops=2 * 128 * 128 * 512,
        name="layer",
    )(
        lengths,
        terms,
        decoded,
        destination.reshape(1, ROWS),
        final_gain.reshape(1, FEAT),
        head_weight.reshape(1, FEAT),
    )
    hidden = lax.all_to_all(placed, fsdp, split_axis=0, concat_axis=0, tiled=True)
    stat = lax.psum(stat[:, :RESP], "tp")
    rewards = lax.rsqrt(stat[0] / D + norm_eps) * stat[1]
    return (hidden, rewards)


def solution(mesh):
    grid = Mesh(mesh.devices.reshape(NT, NZ, NX, NC), ("tp", "z", "x", "core"))
    fsdp = ("z", "x", "core")
    return jax.shard_map(
        body,
        mesh=grid,
        in_specs=(
            P(fsdp, "tp"),
            P(fsdp, None),
            P(fsdp, None),
            P(),
            P(fsdp, "tp"),
            P(fsdp, None),
            P(fsdp, None),
            P("tp", fsdp),
            P("tp"),
            P("tp"),
        ),
        out_specs=(P(fsdp, "tp"), P(fsdp)),
        check_vma=False,
    )
```

```python
import jax
import jax.numpy as jnp
from jax import lax
from jax.experimental import pallas as pl
from jax.experimental.pallas import tpu as pltpu
from jax.sharding import Mesh, PartitionSpec as P

D = 4096
HD = 128
QH = 32
KVH = 2
NT, NZ, NX, NC = 8, 8, 4, 2
ROWS = 128
FEAT = D // NT
BLK = 128
QW = QH * HD // NT
PW = QW + 2 * HD
HEADS = QW // HD
EXTRA = 16
RESP = 8

norm_eps = 1e-06
rope_base = 1000000.0
neg_fill = -1e30

bf16 = jnp.bfloat16
f32 = jnp.float32

VMEM = pl.BlockSpec(memory_space=pltpu.VMEM)
SMEM = pl.BlockSpec(memory_space=pltpu.SMEM)


def call(kernel, out_shape, in_specs, scratch=(), flops=0, name=None):
    return pl.pallas_call(
        kernel,
        out_shape=out_shape,
        in_specs=in_specs,
        out_specs=jax.tree.map(lambda _: VMEM, out_shape),
        scratch_shapes=list(scratch),
        compiler_params=pltpu.CompilerParams(vmem_limit_bytes=24 * 1024 * 1024),
        cost_estimate=pl.CostEstimate(flops=flops, bytes_accessed=4 << 20, transcendentals=0),
        name=name,
    )


def iota(shape, axis):
    return lax.broadcasted_iota(jnp.int32, shape, axis)


def eye_mask():
    return iota((ROWS, ROWS), 0) == iota((ROWS, ROWS), 1)


def resp_starts(lengths_ref, rows):
    end = jnp.int32(0)
    start = jnp.zeros_like(rows)
    for j in range(RESP):
        end = end + lengths_ref[0, j]
        start = jnp.where(rows >= end, end, start)
    return start


def project_kernel(
    place_ref, x_ref, own_ref, other_ref, gain_ref, out0, out1, out2, out3, xs_ref, w_ref
):
    first = place_ref[0] == 0
    outs = (out0, out1, out2, out3)
    for t in range(NT):
        own, other = own_ref[t], other_ref[t]
        w_ref[t * BLK : t * BLK + BLK // 2, :] = jnp.where(first, own, other)
        w_ref[t * BLK + BLK // 2 : (t + 1) * BLK, :] = jnp.where(first, other, own)
    eye = eye_mask()
    for g in range(NX):
        square = jnp.zeros((ROWS, BLK), f32)
        group = lax.rem(place_ref[1] + g, NX)
        for t in range(NT):
            wide = x_ref[t * NX + group].astype(f32)
            square = square + wide * wide
            xs_ref[g * ROWS : (g + 1) * ROWS, t * BLK : (t + 1) * BLK] = (
                wide * gain_ref[t : t + 1, :].astype(f32)
            ).astype(bf16)
        total = jnp.sum(square, axis=1, keepdims=True)
        line = jnp.sum(jnp.where(eye, total, 0.0), axis=0, keepdims=True)
        high = line.astype(bf16).astype(f32)
        low = line - high
        which = iota((EXTRA, ROWS), 0)
        tail = jnp.where(which == 0, high, jnp.where(which == 1, low, 0.0)).astype(bf16)
        outs[g][ROWS:, :] = jnp.concatenate(
            [tail, jnp.zeros((EXTRA, PW - ROWS), bf16)], axis=1
        )
    for n in range(PW // 256):
        cols = slice(n * 256, (n + 1) * 256)
        part = jnp.dot(xs_ref[...], w_ref[:, cols], preferred_element_type=f32)
        for g in range(NX):
            outs[g][:ROWS, cols] = part[g * ROWS : (g + 1) * ROWS].astype(bf16)


def attend_kernel(lengths_ref, part0, part1, part2, part3, freq_ref, out_ref):
    parts = (part0, part1, part2, part3)
    eye = eye_mask()
    line = jnp.zeros((EXTRA, ROWS), f32)
    for i in range(NX):
        line = line + parts[i][ROWS:, :ROWS].astype(f32)
    line = jnp.sum(line, axis=0, keepdims=True)
    total = jnp.sum(jnp.where(eye, line, 0.0), axis=1, keepdims=True)
    scale = lax.rsqrt(total * (1.0 / D) + norm_eps)

    rows = iota((ROWS, ROWS), 0)
    cols = iota((ROWS, ROWS), 1)
    start = resp_starts(lengths_ref, rows)
    allowed = (cols >= start) & (cols <= rows)
    angles = (rows - start).astype(f32) * freq_ref[...]
    cosine = jnp.cos(angles)
    sine = jnp.sin(angles)
    sine = jnp.where(cols < HD // 2, -sine, sine)

    def columns(at):
        summed = parts[0][:ROWS, at : at + HD].astype(f32)
        for part in parts[1:]:
            summed = summed + part[:ROWS, at : at + HD].astype(f32)
        return summed * scale

    def rope(v):
        return (v * cosine + pltpu.roll(v, HD // 2, 1) * sine).astype(bf16)

    keys = rope(columns(QW))
    values = columns(QW + HD).astype(bf16)
    for h in range(HEADS):
        queries = rope(columns(h * HD))
        scores = lax.dot_general(
            queries, keys, (((1,), (1,)), ((), ())), preferred_element_type=f32
        ) * (HD**-0.5)
        scores = jnp.where(allowed, scores, neg_fill)
        top = jnp.max(scores, axis=1, keepdims=True)
        probs = jnp.where(allowed, jnp.exp(scores - top), 0.0)
        sums = jnp.sum(probs, axis=1, keepdims=True)
        weighted = jnp.dot(probs.astype(bf16), values, preferred_element_type=f32)
        out_ref[:, h * HD : (h + 1) * HD] = (weighted / sums).astype(bf16)


def output_kernel(core_ref, x_ref, own_ref, other_ref, out_ref):
    first = core_ref[0] == 0
    for n in range(NT // 2):
        rows = []
        for z in (2 * n, 2 * n + 1):
            own, other = own_ref[z], other_ref[z]
            rows += [jnp.where(first, own, other), jnp.where(first, other, own)]
        part = lax.dot_general(
            x_ref[...],
            jnp.concatenate(rows),
            (((1,), (1,)), ((), ())),
            preferred_element_type=f32,
        )
        for g in range(NX):
            rows = part[g * ROWS : (g + 1) * ROWS].astype(bf16)
            out_ref[2 * n * NX + g] = rows[:, :BLK]
            out_ref[(2 * n + 1) * NX + g] = rows[:, BLK:]


def layer_kernel(lengths_ref, parts_ref, rows_ref, line_ref, final_ref, head_ref, out_ref, stat_ref):
    dest_line = line_ref[...]
    eye = eye_mask()
    dest_column = jnp.sum(jnp.where(eye, dest_line, 0), axis=1, keepdims=True)
    same = (dest_column == dest_line) & (iota((ROWS, ROWS), 0) < iota((ROWS, ROWS), 1))
    rank = jnp.sum(same.astype(jnp.int32), axis=0, keepdims=True)
    slot = dest_line * (ROWS // (NZ * NX * NC)) + rank
    order = (iota((ROWS, ROWS), 0) == slot).astype(f32).astype(bf16)

    square = jnp.zeros((ROWS, BLK), f32)
    product = jnp.zeros((ROWS, BLK), f32)
    for g in range(NX):
        cols = slice(g * BLK, (g + 1) * BLK)
        update = parts_ref[g].astype(f32)
        for t in range(1, NT):
            update = update + parts_ref[t * NX + g].astype(f32)
        layer = (rows_ref[:, cols].astype(f32) + update).astype(bf16)
        wide = layer.astype(f32)
        square = square + wide * wide
        product = product + wide * final_ref[:, cols].astype(f32) * head_ref[:, cols].astype(f32)
        out_ref[:, cols] = jnp.dot(order, layer, preferred_element_type=f32).astype(bf16)

    lane = iota((1, BLK), 1)
    last = jnp.full((1, BLK), -1, jnp.int32)
    end = jnp.int32(0)
    for j in range(RESP):
        end = end + lengths_ref[0, j]
        last = jnp.where(lane == j, end - 1, last)
    pick = iota((ROWS, BLK), 0) == last
    for at, part in ((0, square), (1, product)):
        column = jnp.sum(part, axis=1, keepdims=True)
        stat_ref[at : at + 1, :] = jnp.sum(jnp.where(pick, column, 0.0), axis=0, keepdims=True)


def body(
    decoded,
    lengths,
    destination,
    attn_gain,
    query_weight,
    key_weight,
    value_weight,
    out_weight,
    final_gain,
    head_weight,
):
    me_t, me_x, me_c = lax.axis_index("tp"), lax.axis_index("x"), lax.axis_index("core")
    fsdp = ("z", "x", "core")

    swap = [(0, 1), (1, 0)]
    core = me_c.reshape(1).astype(jnp.int32)

    sent = jnp.broadcast_to(
        decoded.reshape(ROWS, NX, BLK).transpose(1, 0, 2)[None], (NT, NX, ROWS, BLK)
    ).reshape(NT * NX, ROWS, BLK)
    tokens = lax.all_to_all(sent, ("tp", "x"), split_axis=0, concat_axis=0, tiled=True)

    kv_at = me_t // (NT // KVH) * HD
    shard = jnp.concatenate(
        [
            query_weight,
            lax.dynamic_slice_in_dim(key_weight, kv_at, HD, 1),
            lax.dynamic_slice_in_dim(value_weight, kv_at, HD, 1),
        ],
        axis=1,
    )
    own = lax.all_gather(shard, "z", axis=0, tiled=False)
    other = lax.ppermute(own, "core", swap)
    gain = lax.dynamic_slice_in_dim(attn_gain.reshape(NT, NX, BLK), me_x, 1, 1)[:, 0]

    out_sent = jnp.broadcast_to(out_weight.T[None], (NZ,) + out_weight.shape[::-1])
    out_sent, tokens, own = lax.optimization_barrier((out_sent, tokens, own))
    out_own = lax.all_to_all(out_sent, "z", split_axis=0, concat_axis=0, tiled=True)

    block = jax.ShapeDtypeStruct((ROWS + EXTRA, PW), bf16)
    place = jnp.stack([me_c, me_x]).astype(jnp.int32)
    parts = call(
        project_kernel,
        (block,) * NX,
        [SMEM, VMEM, VMEM, VMEM, VMEM],
        [pltpu.VMEM((NX * ROWS, NT * BLK), bf16), pltpu.VMEM((NT * BLK, PW), bf16)],
        flops=2 * 512 * 1024 * 768,
        name="project",
    )(place, tokens, own, other, gain)
    summands = [parts[0]] + [
        lax.ppermute(parts[s], "x", [(i, (i + s) % NX) for i in range(NX)]) for s in range(1, NX)
    ]

    half = jnp.arange(HD // 2, dtype=f32)
    freq = rope_base ** (-(half * 2.0 / HD))
    freq = jnp.concatenate([freq, freq])[None]
    attended = call(
        attend_kernel,
        jax.ShapeDtypeStruct((ROWS, QW), bf16),
        [SMEM] + [VMEM] * (NX + 1),
        flops=2 * 128 * 128 * 128 * 8,
        name="attend",
    )(lengths, *summands, freq)
    out_own, attended = lax.optimization_barrier((out_own, attended))
    out_other = lax.ppermute(out_own, "core", swap)

    slab = lax.all_gather(attended, "x", axis=0, tiled=True)
    products = call(
        output_kernel,
        jax.ShapeDtypeStruct((NT * NX, ROWS, BLK), bf16),
        [SMEM, VMEM, VMEM, VMEM],
        flops=2 * 512 * 512 * 1024,
        name="output",
    )(core, slab, out_own, out_other)
    terms = lax.all_to_all(products, ("tp", "x"), split_axis=0, concat_axis=0, tiled=True)

    placed, stat = call(
        layer_kernel,
        (jax.ShapeDtypeStruct((ROWS, FEAT), bf16), jax.ShapeDtypeStruct((2, BLK), f32)),
        [SMEM, VMEM, VMEM, VMEM, VMEM, VMEM],
        flops=2 * 128 * 128 * 512,
        name="layer",
    )(
        lengths,
        terms,
        decoded,
        destination.reshape(1, ROWS),
        final_gain.reshape(1, FEAT),
        head_weight.reshape(1, FEAT),
    )
    hidden = lax.all_to_all(placed, fsdp, split_axis=0, concat_axis=0, tiled=True)
    stat = lax.psum(stat[:, :RESP], "tp")
    rewards = lax.rsqrt(stat[0] / D + norm_eps) * stat[1]
    return (hidden, rewards)


def solution(mesh):
    grid = Mesh(mesh.devices.reshape(NT, NZ, NX, NC), ("tp", "z", "x", "core"))
    fsdp = ("z", "x", "core")
    return jax.shard_map(
        body,
        mesh=grid,
        in_specs=(
            P(fsdp, "tp"),
            P(fsdp, None),
            P(fsdp, None),
            P(),
            P(fsdp, "tp"),
            P(fsdp, None),
            P(fsdp, None),
            P("tp", fsdp),
            P("tp"),
            P("tp"),
        ),
        out_specs=(P(fsdp, "tp"), P(fsdp)),
        check_vma=False,
    )
```

```python
import jax
import jax.numpy as jnp
from jax import lax
from jax.experimental import pallas as pl
from jax.experimental.pallas import tpu as pltpu
from jax.sharding import Mesh, PartitionSpec as P

D = 4096
HD = 128
QH = 32
KVH = 2
NT, NZ, NX, NC = 8, 8, 4, 2
NQ, NB = 4, 2
TP = ("quad", "pair")
FSDP = ("z", "x", "core")
ORDER = (6, 3, 1, 2, 4, 7, 5, 0)
AT = tuple(ORDER.index(t) for t in range(NT))
ROWS = 128
FEAT = D // NT
BLK = 128
QW = QH * HD // NT
PW = QW + 2 * HD
HEADS = QW // HD
EXTRA = 16
RESP = 8
CAP = 2

norm_eps = 1e-06
rope_base = 1000000.0
neg_fill = -1e30

bf16 = jnp.bfloat16
f32 = jnp.float32

VMEM = pl.BlockSpec(memory_space=pltpu.VMEM)
ANY = pl.BlockSpec(memory_space=pl.ANY)
SMEM = pl.BlockSpec(memory_space=pltpu.SMEM)


def call(kernel, out_shape, in_specs, scratch=(), flops=0, name=None, vmem=24):
    return pl.pallas_call(
        kernel,
        out_shape=out_shape,
        in_specs=in_specs,
        out_specs=jax.tree.map(lambda _: VMEM, out_shape),
        scratch_shapes=list(scratch),
        compiler_params=pltpu.CompilerParams(vmem_limit_bytes=vmem * 1024 * 1024),
        cost_estimate=pl.CostEstimate(flops=flops, bytes_accessed=4 << 20, transcendentals=0),
        name=name,
    )


def iota(shape, axis):
    return lax.broadcasted_iota(jnp.int32, shape, axis)


def eye_mask():
    return iota((ROWS, ROWS), 0) == iota((ROWS, ROWS), 1)


def resp_starts(lengths_ref, rows):
    end = jnp.int32(0)
    start = jnp.zeros_like(rows)
    for j in range(RESP):
        end = end + lengths_ref[0, j]
        start = jnp.where(rows >= end, end, start)
    return start


def prepare_kernel(
    rows, query, key, value, out_w, sent, shard, out_sent, rows_ref, query_ref, kv_ref, out_ref, sems
):
    head = pl.ds(pl.multiple_of(lax.axis_index(TP) // (NT // KVH) * HD, HD), HD)
    moves = (
        (rows, rows_ref),
        (query, query_ref),
        (key.at[:, head], kv_ref.at[0]),
        (value.at[:, head], kv_ref.at[1]),
        (out_w, out_ref),
    )
    copies = [pltpu.make_async_copy(m[0], m[1], sems.at[i]) for i, m in enumerate(moves)]
    for copy in copies:
        copy.start()
    copies[0].wait()
    for g in range(NX):
        block = rows_ref[:, g * BLK : (g + 1) * BLK]
        for t in range(NT):
            sent[t * NX + g] = block
    for copy in copies[1:]:
        copy.wait()
    shard[:, :QW] = query_ref[...]
    shard[:, QW : QW + HD] = kv_ref[0]
    shard[:, QW + HD :] = kv_ref[1]
    for z in range(NZ):
        out_sent[z] = out_ref[...]


def table_kernel(lengths_ref, freq_ref, line_ref, cosine_ref, sine_ref, order_ref):
    rows = iota((ROWS, ROWS), 0)
    cols = iota((ROWS, ROWS), 1)
    angles = (rows - resp_starts(lengths_ref, rows)).astype(f32) * freq_ref[...]
    sine = jnp.sin(angles)
    cosine_ref[...] = jnp.cos(angles)
    sine_ref[...] = jnp.where(cols < HD // 2, -sine, sine)
    dest_line = line_ref[...]
    dest_column = jnp.sum(jnp.where(rows == cols, dest_line, 0), axis=1, keepdims=True)
    same = (dest_column == dest_line) & (rows < cols)
    rank = jnp.sum(same.astype(jnp.int32), axis=0, keepdims=True)
    order_ref[...] = (rows == CAP * dest_line + rank).astype(f32).astype(bf16)


def project_kernel(
    x_ref, own_ref, other_ref, gain_ref, out0, out1, out2, out3, xs_ref, w_ref
):
    first = lax.axis_index("core") == 0
    outs = (out0, out1, out2, out3)
    for t in range(NT):
        own, other = own_ref[t], other_ref[t]
        w_ref[t * BLK : t * BLK + BLK // 2, :] = jnp.where(first, own, other)
        w_ref[t * BLK + BLK // 2 : (t + 1) * BLK, :] = jnp.where(first, other, own)
    eye = eye_mask()
    for g in range(NX):
        square = jnp.zeros((ROWS, BLK), f32)
        group = lax.rem(lax.axis_index("x") + g, NX)
        for t in range(NT):
            wide = x_ref[AT[t] * NX + group].astype(f32)
            square = square + wide * wide
            xs_ref[g * ROWS : (g + 1) * ROWS, t * BLK : (t + 1) * BLK] = (
                wide * gain_ref[t : t + 1, :].astype(f32)
            ).astype(bf16)
        total = jnp.sum(square, axis=1, keepdims=True)
        line = jnp.sum(jnp.where(eye, total, 0.0), axis=0, keepdims=True)
        high = line.astype(bf16).astype(f32)
        low = line - high
        which = iota((EXTRA, ROWS), 0)
        tail = jnp.where(which == 0, high, jnp.where(which == 1, low, 0.0)).astype(bf16)
        outs[g][PW:, :] = tail
    for n in range(PW // 256):
        cols = slice(n * 256, (n + 1) * 256)
        part = jnp.dot(xs_ref[...], w_ref[:, cols], preferred_element_type=f32)
        for g in range(NX):
            rows = part[g * ROWS : (g + 1) * ROWS].astype(bf16)
            outs[g][n * 256 : n * 256 + ROWS, :] = rows[:, :HD]
            outs[g][n * 256 + ROWS : (n + 1) * 256, :] = rows[:, HD:]


def attend_kernel(lengths_ref, part0, part1, part2, part3, cosine_ref, sine_ref, out_ref):
    parts = (part0, part1, part2, part3)
    eye = eye_mask()
    line = jnp.zeros((EXTRA, ROWS), f32)
    for i in range(NX):
        line = line + parts[i][PW:, :].astype(f32)
    line = jnp.sum(line, axis=0, keepdims=True)
    total = jnp.sum(jnp.where(eye, line, 0.0), axis=1, keepdims=True)
    scale = lax.rsqrt(total * (1.0 / D) + norm_eps)

    rows = iota((ROWS, ROWS), 0)
    cols = iota((ROWS, ROWS), 1)
    start = resp_starts(lengths_ref, rows)
    allowed = (cols >= start) & (cols <= rows)
    cosine, sine = cosine_ref[...], sine_ref[...]

    def columns(at):
        summed = parts[0][at : at + HD, :].astype(f32)
        for part in parts[1:]:
            summed = summed + part[at : at + HD, :].astype(f32)
        return summed * scale

    def rope(v):
        return (v * cosine + pltpu.roll(v, HD // 2, 1) * sine).astype(bf16)

    keys = rope(columns(QW))
    values = columns(QW + HD).astype(bf16)
    for h in range(HEADS):
        queries = rope(columns(h * HD))
        scores = lax.dot_general(
            queries, keys, (((1,), (1,)), ((), ())), preferred_element_type=f32
        ) * (HD**-0.5)
        scores = jnp.where(allowed, scores, neg_fill)
        top = jnp.max(scores, axis=1, keepdims=True)
        probs = jnp.where(allowed, jnp.exp(scores - top), 0.0)
        sums = jnp.sum(probs, axis=1, keepdims=True)
        weighted = jnp.dot(probs.astype(bf16), values, preferred_element_type=f32)
        out_ref[:, h * HD : (h + 1) * HD] = (weighted / sums).astype(bf16)


def output_kernel(x_ref, own_ref, other_ref, out_ref):
    first = lax.axis_index("core") == 0
    for n in range(NT // 2):
        rows = []
        for z in (2 * n, 2 * n + 1):
            own, other = own_ref[z], other_ref[z]
            rows += [jnp.where(first, own, other), jnp.where(first, other, own)]
        part = lax.dot_general(
            x_ref[...],
            jnp.concatenate(rows),
            (((1,), (1,)), ((), ())),
            preferred_element_type=f32,
        )
        for g in range(NX):
            rows = part[g * ROWS : (g + 1) * ROWS].astype(bf16)
            out_ref[AT[2 * n] * NX + g] = rows[:, :BLK]
            out_ref[AT[2 * n + 1] * NX + g] = rows[:, BLK:]


def layer_kernel(
    lengths_ref, parts_ref, rows_ref, order_ref, final_ref, head_ref, out_ref, stat_ref
):
    square = jnp.zeros((ROWS, BLK), f32)
    product = jnp.zeros((ROWS, BLK), f32)
    for g in range(NX):
        cols = slice(g * BLK, (g + 1) * BLK)
        update = parts_ref[g].astype(f32)
        for t in range(1, NT):
            update = update + parts_ref[t * NX + g].astype(f32)
        layer = (rows_ref[:, cols].astype(f32) + update).astype(bf16)
        wide = layer.astype(f32)
        square = square + wide * wide
        product = product + wide * final_ref[:, cols].astype(f32) * head_ref[:, cols].astype(f32)
        out_ref[:, cols] = jnp.dot(order_ref[...], layer, preferred_element_type=f32).astype(bf16)

    lane = iota((1, BLK), 1)
    last = jnp.full((1, BLK), -1, jnp.int32)
    end = jnp.int32(0)
    for j in range(RESP):
        end = end + lengths_ref[0, j]
        last = jnp.where(lane == j, end - 1, last)
    pick = iota((ROWS, BLK), 0) == last
    for at, part in ((0, square), (1, product)):
        column = jnp.sum(part, axis=1, keepdims=True)
        stat_ref[at : at + 1, :] = jnp.sum(jnp.where(pick, column, 0.0), axis=0, keepdims=True)


def exchange(blocks):
    return lax.all_to_all(
        blocks,
        TP + ("x",),
        split_axis=0,
        concat_axis=0,
        tiled=True,
        axis_index_groups=[[t * NX + g for t in ORDER for g in range(NX)]],
    )


def body(
    decoded,
    lengths,
    destination,
    attn_gain,
    query_weight,
    key_weight,
    value_weight,
    out_weight,
    final_gain,
    head_weight,
):
    me_x = lax.axis_index("x")
    swap = [(0, 1), (1, 0)]

    sent, shard, out_sent = call(
        prepare_kernel,
        (
            jax.ShapeDtypeStruct((NT * NX, ROWS, BLK), bf16),
            jax.ShapeDtypeStruct((D // (NZ * NX * NC), PW), bf16),
            jax.ShapeDtypeStruct((NZ, D // (NZ * NX * NC), QW), bf16),
        ),
        [ANY] * 5,
        [
            pltpu.VMEM((ROWS, FEAT), bf16),
            pltpu.VMEM((D // (NZ * NX * NC), QW), bf16),
            pltpu.VMEM((2, D // (NZ * NX * NC), HD), bf16),
            pltpu.VMEM((D // (NZ * NX * NC), QW), bf16),
            pltpu.SemaphoreType.DMA((5,)),
        ],
        name="prepare",
        vmem=60,
    )(decoded, query_weight, key_weight, value_weight, out_weight.T)
    tokens = exchange(sent)
    own = lax.all_gather(shard, "z", axis=0, tiled=False)
    other = lax.ppermute(own, "core", swap)
    gain = lax.dynamic_slice_in_dim(attn_gain.reshape(NT, NX, BLK), me_x, 1, 1)[:, 0]

    out_sent, tokens, own = lax.optimization_barrier((out_sent, tokens, own))
    out_own = lax.all_to_all(out_sent, "z", split_axis=0, concat_axis=0, tiled=True)

    block = jax.ShapeDtypeStruct((PW + EXTRA, HD), bf16)
    parts = call(
        project_kernel,
        (block,) * NX,
        [VMEM] * 4,
        [pltpu.VMEM((NX * ROWS, NT * BLK), bf16), pltpu.VMEM((NT * BLK, PW), bf16)],
        flops=2 * 512 * 1024 * 768,
        name="project",
    )(tokens, own, other, gain)
    summands = [parts[0]] + [
        lax.ppermute(parts[s], "x", [(i, (i + s) % NX) for i in range(NX)]) for s in range(1, NX)
    ]

    half = jnp.arange(HD // 2, dtype=f32)
    freq = rope_base ** (-(half * 2.0 / HD))
    freq = jnp.concatenate([freq, freq])[None]
    own_part, after, line = lax.optimization_barrier(
        (summands[0], lengths, destination.reshape(1, ROWS))
    )
    cosine, sine, order = call(
        table_kernel,
        (jax.ShapeDtypeStruct((ROWS, HD), f32),) * 2 + (jax.ShapeDtypeStruct((ROWS, ROWS), bf16),),
        [SMEM, VMEM, VMEM],
        name="tables",
    )(after, freq, line)
    attended = call(
        attend_kernel,
        jax.ShapeDtypeStruct((ROWS, QW), bf16),
        [SMEM] + [VMEM] * (NX + 2),
        flops=2 * 128 * 128 * 128 * 8,
        name="attend",
    )(lengths, own_part, *summands[1:], cosine, sine)
    out_own, attended = lax.optimization_barrier((out_own, attended))
    out_other = lax.ppermute(out_own, "core", swap)

    slab = lax.all_gather(attended, "x", axis=0, tiled=True)
    products = call(
        output_kernel,
        jax.ShapeDtypeStruct((NT * NX, ROWS, BLK), bf16),
        [VMEM] * 3,
        flops=2 * 512 * 512 * 1024,
        name="output",
    )(slab, out_own, out_other)
    terms = exchange(products)

    placed, stat = call(
        layer_kernel,
        (
            jax.ShapeDtypeStruct((ROWS, FEAT), bf16),
            jax.ShapeDtypeStruct((2, BLK), f32),
        ),
        [SMEM] + [VMEM] * 5,
        flops=2 * 128 * 128 * 512,
        name="layer",
    )(
        lengths,
        terms,
        decoded,
        order,
        final_gain.reshape(1, FEAT),
        head_weight.reshape(1, FEAT),
    )
    hidden = lax.all_to_all(placed, FSDP, split_axis=0, concat_axis=0, tiled=True)
    stat = lax.psum(stat[:, :RESP], TP)
    rewards = lax.rsqrt(stat[0] / D + norm_eps) * stat[1]
    return (hidden, rewards)


def solution(mesh):
    grid = Mesh(mesh.devices.reshape(NQ, NB, NZ, NX, NC), TP + FSDP)
    return jax.shard_map(
        body,
        mesh=grid,
        in_specs=(
            P(FSDP, TP),
            P(FSDP, None),
            P(FSDP, None),
            P(),
            P(FSDP, TP),
            P(FSDP, None),
            P(FSDP, None),
            P(TP, FSDP),
            P(TP),
            P(TP),
        ),
        out_specs=(P(FSDP, TP), P(FSDP)),
        check_vma=False,
    )
```

```python
import jax
import jax.numpy as jnp
from jax import lax
from jax.experimental import pallas as pl
from jax.experimental.pallas import tpu as pltpu
from jax.sharding import Mesh, PartitionSpec as P

D = 4096
HD = 128
QH = 32
KVH = 2
NT, NZ, NX, NC = 8, 8, 4, 2
NQ, NB = 4, 2
TP = ("tp",)
Z = ("quad", "pair")
FSDP = Z + ("x", "core")
ORDER = (6, 3, 1, 2, 4, 7, 5, 0)
AT = tuple(ORDER.index(t) for t in range(NT))
ROWS = 128
FEAT = D // NT
BLK = 128
QW = QH * HD // NT
PW = QW + 2 * HD
HEADS = QW // HD
EXTRA = 16
RESP = 8
CAP = 2

norm_eps = 1e-06
rope_base = 1000000.0
neg_fill = -1e30

bf16 = jnp.bfloat16
f32 = jnp.float32

VMEM = pl.BlockSpec(memory_space=pltpu.VMEM)
ANY = pl.BlockSpec(memory_space=pl.ANY)
SMEM = pl.BlockSpec(memory_space=pltpu.SMEM)


def call(kernel, out_shape, in_specs, scratch=(), flops=0, name=None, vmem=24):
    return pl.pallas_call(
        kernel,
        out_shape=out_shape,
        in_specs=in_specs,
        out_specs=jax.tree.map(lambda _: VMEM, out_shape),
        scratch_shapes=list(scratch),
        compiler_params=pltpu.CompilerParams(vmem_limit_bytes=vmem * 1024 * 1024),
        cost_estimate=pl.CostEstimate(flops=flops, bytes_accessed=4 << 20, transcendentals=0),
        name=name,
    )


def iota(shape, axis):
    return lax.broadcasted_iota(jnp.int32, shape, axis)


def eye_mask():
    return iota((ROWS, ROWS), 0) == iota((ROWS, ROWS), 1)


def resp_starts(lengths_ref, rows):
    end = jnp.int32(0)
    start = jnp.zeros_like(rows)
    for j in range(RESP):
        end = end + lengths_ref[0, j]
        start = jnp.where(rows >= end, end, start)
    return start


def prepare_kernel(
    rows, query, key, value, out_w, sent, shard, out_sent, rows_ref, query_ref, kv_ref, out_ref, sems
):
    head = pl.ds(pl.multiple_of(lax.axis_index(TP) // (NT // KVH) * HD, HD), HD)
    moves = (
        (rows, rows_ref),
        (query, query_ref),
        (key.at[:, head], kv_ref.at[0]),
        (value.at[:, head], kv_ref.at[1]),
        (out_w, out_ref),
    )
    copies = [pltpu.make_async_copy(m[0], m[1], sems.at[i]) for i, m in enumerate(moves)]
    for copy in copies:
        copy.start()
    copies[0].wait()
    for g in range(NX):
        block = rows_ref[:, g * BLK : (g + 1) * BLK]
        for t in range(NT):
            sent[t * NX + g] = block
    for copy in copies[1:]:
        copy.wait()
    shard[:, :QW] = query_ref[...]
    shard[:, QW : QW + HD] = kv_ref[0]
    shard[:, QW + HD :] = kv_ref[1]
    for z in range(NZ):
        out_sent[z] = out_ref[...]


def table_kernel(lengths_ref, freq_ref, line_ref, cosine_ref, sine_ref, order_ref):
    rows = iota((ROWS, ROWS), 0)
    cols = iota((ROWS, ROWS), 1)
    angles = (rows - resp_starts(lengths_ref, rows)).astype(f32) * freq_ref[...]
    sine = jnp.sin(angles)
    cosine_ref[...] = jnp.cos(angles)
    sine_ref[...] = jnp.where(cols < HD // 2, -sine, sine)
    dest_line = line_ref[...]
    dest_column = jnp.sum(jnp.where(rows == cols, dest_line, 0), axis=1, keepdims=True)
    same = (dest_column == dest_line) & (rows < cols)
    rank = jnp.sum(same.astype(jnp.int32), axis=0, keepdims=True)
    z, x, c = dest_line // (NX * NC), dest_line // NC % NX, dest_line % NC
    place = (x * NZ + z) * NC + c
    order_ref[...] = (rows == CAP * place + rank).astype(f32).astype(bf16)


def project_kernel(
    x_ref, own_ref, other_ref, gain_ref, out0, out1, out2, out3, xs_ref, w_ref
):
    first = lax.axis_index("core") == 0
    outs = (out0, out1, out2, out3)
    for t in range(NT):
        own, other = own_ref[t], other_ref[t]
        w_ref[t * BLK : t * BLK + BLK // 2, :] = jnp.where(first, own, other)
        w_ref[t * BLK + BLK // 2 : (t + 1) * BLK, :] = jnp.where(first, other, own)
    eye = eye_mask()
    for g in range(NX):
        square = jnp.zeros((ROWS, BLK), f32)
        group = lax.rem(lax.axis_index("x") + g, NX)
        for t in range(NT):
            wide = x_ref[AT[t] * NX + group].astype(f32)
            square = square + wide * wide
            xs_ref[g * ROWS : (g + 1) * ROWS, t * BLK : (t + 1) * BLK] = (
                wide * gain_ref[t : t + 1, :].astype(f32)
            ).astype(bf16)
        total = jnp.sum(square, axis=1, keepdims=True)
        line = jnp.sum(jnp.where(eye, total, 0.0), axis=0, keepdims=True)
        high = line.astype(bf16).astype(f32)
        low = line - high
        which = iota((EXTRA, ROWS), 0)
        tail = jnp.where(which == 0, high, jnp.where(which == 1, low, 0.0)).astype(bf16)
        outs[g][PW:, :] = tail
    for n in range(PW // 256):
        cols = slice(n * 256, (n + 1) * 256)
        part = jnp.dot(xs_ref[...], w_ref[:, cols], preferred_element_type=f32)
        for g in range(NX):
            rows = part[g * ROWS : (g + 1) * ROWS].astype(bf16)
            outs[g][n * 256 : n * 256 + ROWS, :] = rows[:, :HD]
            outs[g][n * 256 + ROWS : (n + 1) * 256, :] = rows[:, HD:]


def attend_kernel(lengths_ref, part0, part1, part2, part3, cosine_ref, sine_ref, out_ref):
    parts = (part0, part1, part2, part3)
    eye = eye_mask()
    line = jnp.zeros((EXTRA, ROWS), f32)
    for i in range(NX):
        line = line + parts[i][PW:, :].astype(f32)
    line = jnp.sum(line, axis=0, keepdims=True)
    total = jnp.sum(jnp.where(eye, line, 0.0), axis=1, keepdims=True)
    scale = lax.rsqrt(total * (1.0 / D) + norm_eps)

    rows = iota((ROWS, ROWS), 0)
    cols = iota((ROWS, ROWS), 1)
    start = resp_starts(lengths_ref, rows)
    allowed = (cols >= start) & (cols <= rows)
    cosine, sine = cosine_ref[...], sine_ref[...]

    def columns(at):
        summed = parts[0][at : at + HD, :].astype(f32)
        for part in parts[1:]:
            summed = summed + part[at : at + HD, :].astype(f32)
        return summed * scale

    def rope(v):
        return (v * cosine + pltpu.roll(v, HD // 2, 1) * sine).astype(bf16)

    keys = rope(columns(QW))
    values = columns(QW + HD).astype(bf16)
    for h in range(HEADS):
        queries = rope(columns(h * HD))
        scores = lax.dot_general(
            queries, keys, (((1,), (1,)), ((), ())), preferred_element_type=f32
        ) * (HD**-0.5)
        scores = jnp.where(allowed, scores, neg_fill)
        top = jnp.max(scores, axis=1, keepdims=True)
        probs = jnp.where(allowed, jnp.exp(scores - top), 0.0)
        sums = jnp.sum(probs, axis=1, keepdims=True)
        weighted = jnp.dot(probs.astype(bf16), values, preferred_element_type=f32)
        out_ref[:, h * HD : (h + 1) * HD] = (weighted / sums).astype(bf16)


def output_kernel(x_ref, own_ref, other_ref, out_ref):
    first = lax.axis_index("core") == 0
    for n in range(NT // 2):
        rows = []
        for z in (2 * n, 2 * n + 1):
            own, other = own_ref[z], other_ref[z]
            rows += [jnp.where(first, own, other), jnp.where(first, other, own)]
        part = lax.dot_general(
            x_ref[...],
            jnp.concatenate(rows),
            (((1,), (1,)), ((), ())),
            preferred_element_type=f32,
        )
        for g in range(NX):
            rows = part[g * ROWS : (g + 1) * ROWS].astype(bf16)
            out_ref[AT[2 * n] * NX + g] = rows[:, :BLK]
            out_ref[AT[2 * n + 1] * NX + g] = rows[:, BLK:]


def layer_kernel(
    lengths_ref, parts_ref, rows_ref, order_ref, final_ref, head_ref, out_ref, stat_ref
):
    square = jnp.zeros((ROWS, BLK), f32)
    product = jnp.zeros((ROWS, BLK), f32)
    for g in range(NX):
        cols = slice(g * BLK, (g + 1) * BLK)
        update = parts_ref[g].astype(f32)
        for t in range(1, NT):
            update = update + parts_ref[t * NX + g].astype(f32)
        layer = (rows_ref[:, cols].astype(f32) + update).astype(bf16)
        wide = layer.astype(f32)
        square = square + wide * wide
        product = product + wide * final_ref[:, cols].astype(f32) * head_ref[:, cols].astype(f32)
        out_ref[:, cols] = jnp.dot(order_ref[...], layer, preferred_element_type=f32).astype(bf16)

    lane = iota((1, BLK), 1)
    last = jnp.full((1, BLK), -1, jnp.int32)
    end = jnp.int32(0)
    for j in range(RESP):
        end = end + lengths_ref[0, j]
        last = jnp.where(lane == j, end - 1, last)
    pick = iota((ROWS, BLK), 0) == last
    for at, part in ((0, square), (1, product)):
        column = jnp.sum(part, axis=1, keepdims=True)
        stat_ref[at : at + 1, :] = jnp.sum(jnp.where(pick, column, 0.0), axis=0, keepdims=True)


def exchange(blocks):
    return lax.all_to_all(
        blocks,
        TP + ("x",),
        split_axis=0,
        concat_axis=0,
        tiled=True,
        axis_index_groups=[[t * NX + g for t in ORDER for g in range(NX)]],
    )


def body(
    decoded,
    lengths,
    destination,
    attn_gain,
    query_weight,
    key_weight,
    value_weight,
    out_weight,
    final_gain,
    head_weight,
):
    me_x = lax.axis_index("x")
    swap = [(0, 1), (1, 0)]

    sent, shard, out_sent = call(
        prepare_kernel,
        (
            jax.ShapeDtypeStruct((NT * NX, ROWS, BLK), bf16),
            jax.ShapeDtypeStruct((D // (NZ * NX * NC), PW), bf16),
            jax.ShapeDtypeStruct((NZ, D // (NZ * NX * NC), QW), bf16),
        ),
        [ANY] * 5,
        [
            pltpu.VMEM((ROWS, FEAT), bf16),
            pltpu.VMEM((D // (NZ * NX * NC), QW), bf16),
            pltpu.VMEM((2, D // (NZ * NX * NC), HD), bf16),
            pltpu.VMEM((D // (NZ * NX * NC), QW), bf16),
            pltpu.SemaphoreType.DMA((5,)),
        ],
        name="prepare",
        vmem=60,
    )(decoded, query_weight, key_weight, value_weight, out_weight.T)
    tokens = exchange(sent)
    own = lax.all_gather(lax.all_gather(shard, "pair"), "quad")
    own = own.reshape((NZ,) + shard.shape)
    other = lax.ppermute(own, "core", swap)
    gain = lax.dynamic_slice_in_dim(attn_gain.reshape(NT, NX, BLK), me_x, 1, 1)[:, 0]

    out_sent, tokens, own = lax.optimization_barrier((out_sent, tokens, own))
    out_own = lax.all_to_all(out_sent, Z, split_axis=0, concat_axis=0, tiled=True)

    block = jax.ShapeDtypeStruct((PW + EXTRA, HD), bf16)
    parts = call(
        project_kernel,
        (block,) * NX,
        [VMEM] * 4,
        [pltpu.VMEM((NX * ROWS, NT * BLK), bf16), pltpu.VMEM((NT * BLK, PW), bf16)],
        flops=2 * 512 * 1024 * 768,
        name="project",
    )(tokens, own, other, gain)
    summands = [parts[0]] + [
        lax.ppermute(parts[s], "x", [(i, (i + s) % NX) for i in range(NX)]) for s in (2, 1, 3)
    ]

    half = jnp.arange(HD // 2, dtype=f32)
    freq = rope_base ** (-(half * 2.0 / HD))
    freq = jnp.concatenate([freq, freq])[None]
    own_part, after, line = lax.optimization_barrier(
        (summands[0], lengths, destination.reshape(1, ROWS))
    )
    cosine, sine, order = call(
        table_kernel,
        (jax.ShapeDtypeStruct((ROWS, HD), f32),) * 2 + (jax.ShapeDtypeStruct((ROWS, ROWS), bf16),),
        [SMEM, VMEM, VMEM],
        name="tables",
    )(after, freq, line)
    attended = call(
        attend_kernel,
        jax.ShapeDtypeStruct((ROWS, QW), bf16),
        [SMEM] + [VMEM] * (NX + 2),
        flops=2 * 128 * 128 * 128 * 8,
        name="attend",
    )(lengths, own_part, *summands[1:], cosine, sine)

    out_own, attended = lax.optimization_barrier((out_own, attended))
    out_other = lax.ppermute(out_own, "core", swap)

    slab = lax.all_gather(attended, "x", axis=0, tiled=True)
    products = call(
        output_kernel,
        jax.ShapeDtypeStruct((NT * NX, ROWS, BLK), bf16),
        [VMEM] * 3,
        flops=2 * 512 * 512 * 1024,
        name="output",
    )(slab, out_own, out_other)
    terms = exchange(products)

    placed, stat = call(
        layer_kernel,
        (
            jax.ShapeDtypeStruct((ROWS, FEAT), bf16),
            jax.ShapeDtypeStruct((2, BLK), f32),
        ),
        [SMEM] + [VMEM] * 5,
        flops=2 * 128 * 128 * 512,
        name="layer",
    )(
        lengths,
        terms,
        decoded,
        order,
        final_gain.reshape(1, FEAT),
        head_weight.reshape(1, FEAT),
    )
    hidden = lax.all_to_all(placed, ("x",) + Z + ("core",), split_axis=0, concat_axis=0, tiled=True)
    hidden = hidden.reshape(NX, NZ, NC * CAP, FEAT).transpose(1, 0, 2, 3).reshape(ROWS, FEAT)
    stat = lax.psum(stat[:, :RESP], TP)
    rewards = lax.rsqrt(stat[0] / D + norm_eps) * stat[1]
    return (hidden, rewards)


def solution(mesh):
    grid = Mesh(mesh.devices.reshape(NT, NQ, NB, NX, NC), TP + FSDP)
    return jax.shard_map(
        body,
        mesh=grid,
        in_specs=(
            P(FSDP, TP),
            P(FSDP, None),
            P(FSDP, None),
            P(),
            P(FSDP, TP),
            P(FSDP, None),
            P(FSDP, None),
            P(TP, FSDP),
            P(TP),
            P(TP),
        ),
        out_specs=(P(FSDP, TP), P(FSDP)),
        check_vma=False,
    )
```

```python
import jax
import jax.numpy as jnp
from jax import lax
from jax.experimental import pallas as pl
from jax.experimental.pallas import tpu as pltpu
from jax.sharding import Mesh, PartitionSpec as P

D = 4096
HD = 128
QH = 32
KVH = 2
NT, NZ, NX, NC = 8, 8, 4, 2
NQ, NB = 4, 2
TP = ("four", "two")
Z = ("quad", "pair")
FSDP = Z + ("x", "core")
ORDER = (6, 3, 1, 2, 4, 7, 5, 0)
AT = tuple(ORDER.index(t) for t in range(NT))
ROWS = 128
FEAT = D // NT
BLK = 128
QW = QH * HD // NT
PW = QW + 2 * HD
HEADS = QW // HD
HALF = ROWS // NB
EXTRA = 16
RESP = 8
CAP = 2

norm_eps = 1e-06
rope_base = 1000000.0
neg_fill = -1e30

bf16 = jnp.bfloat16
f32 = jnp.float32

VMEM = pl.BlockSpec(memory_space=pltpu.VMEM)
ANY = pl.BlockSpec(memory_space=pl.ANY)
SMEM = pl.BlockSpec(memory_space=pltpu.SMEM)


def call(kernel, out_shape, in_specs, scratch=(), flops=0, name=None, vmem=24):
    return pl.pallas_call(
        kernel,
        out_shape=out_shape,
        in_specs=in_specs,
        out_specs=jax.tree.map(lambda _: VMEM, out_shape),
        scratch_shapes=list(scratch),
        compiler_params=pltpu.CompilerParams(vmem_limit_bytes=vmem * 1024 * 1024),
        cost_estimate=pl.CostEstimate(flops=flops, bytes_accessed=4 << 20, transcendentals=0),
        name=name,
    )


def iota(shape, axis):
    return lax.broadcasted_iota(jnp.int32, shape, axis)


def eye_mask():
    return iota((ROWS, ROWS), 0) == iota((ROWS, ROWS), 1)


def resp_starts(lengths_ref, rows):
    end = jnp.int32(0)
    start = jnp.zeros_like(rows)
    for j in range(RESP):
        end = end + lengths_ref[0, j]
        start = jnp.where(rows >= end, end, start)
    return start


def prepare_kernel(
    rows, query, key, value, out_w, sent, shard, out_sent, rows_ref, query_ref, kv_ref, out_ref, sems
):
    head = pl.ds(pl.multiple_of(lax.axis_index(TP) // (NT // KVH) * HD, HD), HD)
    moves = (
        (rows, rows_ref),
        (query, query_ref),
        (key.at[:, head], kv_ref.at[0]),
        (value.at[:, head], kv_ref.at[1]),
        (out_w, out_ref),
    )
    copies = [pltpu.make_async_copy(m[0], m[1], sems.at[i]) for i, m in enumerate(moves)]
    for copy in copies:
        copy.start()
    copies[0].wait()
    for g in range(NX):
        block = rows_ref[:, g * BLK : (g + 1) * BLK]
        for t in range(NT):
            sent[t * NX + g] = block
    for copy in copies[1:]:
        copy.wait()
    shard[:, :QW] = query_ref[...]
    shard[:, QW : QW + HD] = kv_ref[0]
    shard[:, QW + HD :] = kv_ref[1]
    for i in range(NB * NZ):
        out_sent[i] = out_ref[...]


def table_kernel(lengths_ref, freq_ref, line_ref, cosine_ref, sine_ref, order_ref):
    rows = iota((ROWS, ROWS), 0)
    cols = iota((ROWS, ROWS), 1)
    angles = (rows - resp_starts(lengths_ref, rows)).astype(f32) * freq_ref[...]
    sine = jnp.sin(angles)
    cosine_ref[...] = jnp.cos(angles)
    sine_ref[...] = jnp.where(cols < HD // 2, -sine, sine)
    dest_line = line_ref[...]
    dest_column = jnp.sum(jnp.where(rows == cols, dest_line, 0), axis=1, keepdims=True)
    same = (dest_column == dest_line) & (rows < cols)
    rank = jnp.sum(same.astype(jnp.int32), axis=0, keepdims=True)
    z, x, c = dest_line // (NX * NC), dest_line // NC % NX, dest_line % NC
    place = (x * NZ + z) * NC + c
    order_ref[...] = (rows == CAP * place + rank).astype(f32).astype(bf16)


def project_kernel(
    x_ref, own_ref, other_ref, gain_ref, out0, out1, out2, out3, xs_ref, w_ref
):
    first = lax.axis_index("core") == 0
    outs = (out0, out1, out2, out3)
    for t in range(NT):
        own, other = own_ref[t], other_ref[t]
        w_ref[t * BLK : t * BLK + BLK // 2, :] = jnp.where(first, own, other)
        w_ref[t * BLK + BLK // 2 : (t + 1) * BLK, :] = jnp.where(first, other, own)
    eye = eye_mask()
    for g in range(NX):
        square = jnp.zeros((ROWS, BLK), f32)
        group = lax.rem(lax.axis_index("x") + g, NX)
        for t in range(NT):
            wide = x_ref[AT[t] * NX + group].astype(f32)
            square = square + wide * wide
            xs_ref[g * ROWS : (g + 1) * ROWS, t * BLK : (t + 1) * BLK] = (
                wide * gain_ref[t : t + 1, :].astype(f32)
            ).astype(bf16)
        total = jnp.sum(square, axis=1, keepdims=True)
        line = jnp.sum(jnp.where(eye, total, 0.0), axis=0, keepdims=True)
        high = line.astype(bf16).astype(f32)
        low = line - high
        which = iota((EXTRA, ROWS), 0)
        tail = jnp.where(which == 0, high, jnp.where(which == 1, low, 0.0)).astype(bf16)
        outs[g][PW:, :] = tail
    for n in range(PW // 256):
        cols = slice(n * 256, (n + 1) * 256)
        part = jnp.dot(xs_ref[...], w_ref[:, cols], preferred_element_type=f32)
        for g in range(NX):
            rows = part[g * ROWS : (g + 1) * ROWS].astype(bf16)
            outs[g][n * 256 : n * 256 + ROWS, :] = rows[:, :HD]
            outs[g][n * 256 + ROWS : (n + 1) * 256, :] = rows[:, HD:]


def attend_kernel(lengths_ref, part0, part1, part2, part3, cosine_ref, sine_ref, out_ref):
    parts = (part0, part1, part2, part3)
    eye = eye_mask()
    line = jnp.zeros((EXTRA, ROWS), f32)
    for i in range(NX):
        line = line + parts[i][PW:, :].astype(f32)
    line = jnp.sum(line, axis=0, keepdims=True)
    total = jnp.sum(jnp.where(eye, line, 0.0), axis=1, keepdims=True)
    scale = lax.rsqrt(total * (1.0 / D) + norm_eps)

    rows = iota((ROWS, ROWS), 0)
    cols = iota((ROWS, ROWS), 1)
    start = resp_starts(lengths_ref, rows)
    allowed = (cols >= start) & (cols <= rows)
    cosine, sine = cosine_ref[...], sine_ref[...]

    def columns(at):
        summed = parts[0][at : at + HD, :].astype(f32)
        for part in parts[1:]:
            summed = summed + part[at : at + HD, :].astype(f32)
        return summed * scale

    def rope(v):
        return (v * cosine + pltpu.roll(v, HD // 2, 1) * sine).astype(bf16)

    keys = rope(columns(QW))
    values = columns(QW + HD).astype(bf16)
    for h in range(HEADS):
        queries = rope(columns(h * HD))
        scores = lax.dot_general(
            queries, keys, (((1,), (1,)), ((), ())), preferred_element_type=f32
        ) * (HD**-0.5)
        scores = jnp.where(allowed, scores, neg_fill)
        top = jnp.max(scores, axis=1, keepdims=True)
        probs = jnp.where(allowed, jnp.exp(scores - top), 0.0)
        sums = jnp.sum(probs, axis=1, keepdims=True)
        weighted = jnp.dot(probs.astype(bf16), values, preferred_element_type=f32)
        result = (weighted / sums).astype(bf16)
        for b in range(NB):
            for g in range(NX):
                out_ref[b * NX + g, :, h * HD : (h + 1) * HD] = result[b * HALF : (b + 1) * HALF]


def output_kernel(x_ref, own_ref, other_ref, out_ref):
    first = lax.axis_index("core") == 0
    for n in range(NT // 2):
        part = None
        for b in range(NB):
            rows = []
            for z in (2 * n, 2 * n + 1):
                own, other = own_ref[b * NZ + z], other_ref[b * NZ + z]
                rows += [jnp.where(first, own, other), jnp.where(first, other, own)]
            x = x_ref[b * NX : (b + 1) * NX].reshape(NX * HALF, QW)
            term = lax.dot_general(
                x,
                jnp.concatenate(rows),
                (((1,), (1,)), ((), ())),
                preferred_element_type=f32,
            )
            part = term if part is None else part + term
        for g in range(NX):
            rows = part[g * HALF : (g + 1) * HALF].astype(bf16)
            out_ref[AT[2 * n] * NX + g] = rows[:, :BLK]
            out_ref[AT[2 * n + 1] * NX + g] = rows[:, BLK:]


def layer_kernel(
    lengths_ref, parts_ref, rows_ref, order_ref, final_ref, head_ref, out_ref, stat_ref
):
    square = jnp.zeros((ROWS, BLK), f32)
    product = jnp.zeros((ROWS, BLK), f32)
    for g in range(NX):
        cols = slice(g * BLK, (g + 1) * BLK)
        halves = []
        for b in range(NB):
            half = parts_ref[AT[b] * NX + g].astype(f32)
            for t in range(b + NB, NT, NB):
                half = half + parts_ref[AT[t] * NX + g].astype(f32)
            halves.append(half)
        update = jnp.concatenate(halves)
        layer = (rows_ref[:, cols].astype(f32) + update).astype(bf16)
        wide = layer.astype(f32)
        square = square + wide * wide
        product = product + wide * final_ref[:, cols].astype(f32) * head_ref[:, cols].astype(f32)
        out_ref[:, cols] = jnp.dot(order_ref[...], layer, preferred_element_type=f32).astype(bf16)

    lane = iota((1, BLK), 1)
    last = jnp.full((1, BLK), -1, jnp.int32)
    end = jnp.int32(0)
    for j in range(RESP):
        end = end + lengths_ref[0, j]
        last = jnp.where(lane == j, end - 1, last)
    pick = iota((ROWS, BLK), 0) == last
    for at, part in ((0, square), (1, product)):
        column = jnp.sum(part, axis=1, keepdims=True)
        stat_ref[at : at + 1, :] = jnp.sum(jnp.where(pick, column, 0.0), axis=0, keepdims=True)


def exchange(blocks):
    return lax.all_to_all(
        blocks,
        TP + ("x",),
        split_axis=0,
        concat_axis=0,
        tiled=True,
        axis_index_groups=[[t * NX + g for t in ORDER for g in range(NX)]],
    )


def body(
    decoded,
    lengths,
    destination,
    attn_gain,
    query_weight,
    key_weight,
    value_weight,
    out_weight,
    final_gain,
    head_weight,
):
    me_x = lax.axis_index("x")
    swap = [(0, 1), (1, 0)]

    sent, shard, out_sent = call(
        prepare_kernel,
        (
            jax.ShapeDtypeStruct((NT * NX, ROWS, BLK), bf16),
            jax.ShapeDtypeStruct((D // (NZ * NX * NC), PW), bf16),
            jax.ShapeDtypeStruct((NB * NZ, D // (NZ * NX * NC), QW), bf16),
        ),
        [ANY] * 5,
        [
            pltpu.VMEM((ROWS, FEAT), bf16),
            pltpu.VMEM((D // (NZ * NX * NC), QW), bf16),
            pltpu.VMEM((2, D // (NZ * NX * NC), HD), bf16),
            pltpu.VMEM((D // (NZ * NX * NC), QW), bf16),
            pltpu.SemaphoreType.DMA((5,)),
        ],
        name="prepare",
        vmem=60,
    )(decoded, query_weight, key_weight, value_weight, out_weight.T)
    tokens = exchange(sent)
    own = lax.all_gather(lax.all_gather(shard, "pair"), "quad")
    own = own.reshape((NZ,) + shard.shape)
    other = lax.ppermute(own, "core", swap)
    gain = lax.dynamic_slice_in_dim(attn_gain.reshape(NT, NX, BLK), me_x, 1, 1)[:, 0]

    out_sent, tokens, own = lax.optimization_barrier((out_sent, tokens, own))
    out_own = lax.all_to_all(out_sent, ("two",) + Z, split_axis=0, concat_axis=0, tiled=True)

    block = jax.ShapeDtypeStruct((PW + EXTRA, HD), bf16)
    parts = call(
        project_kernel,
        (block,) * NX,
        [VMEM] * 4,
        [pltpu.VMEM((NX * ROWS, NT * BLK), bf16), pltpu.VMEM((NT * BLK, PW), bf16)],
        flops=2 * 512 * 1024 * 768,
        name="project",
    )(tokens, own, other, gain)
    summands = [parts[0]] + [
        lax.ppermute(parts[s], "x", [(i, (i + s) % NX) for i in range(NX)]) for s in (2, 1, 3)
    ]

    half = jnp.arange(HD // 2, dtype=f32)
    freq = rope_base ** (-(half * 2.0 / HD))
    freq = jnp.concatenate([freq, freq])[None]
    own_part, after, line = lax.optimization_barrier(
        (summands[0], lengths, destination.reshape(1, ROWS))
    )
    cosine, sine, order = call(
        table_kernel,
        (jax.ShapeDtypeStruct((ROWS, HD), f32),) * 2 + (jax.ShapeDtypeStruct((ROWS, ROWS), bf16),),
        [SMEM, VMEM, VMEM],
        name="tables",
    )(after, freq, line)
    attended = call(
        attend_kernel,
        jax.ShapeDtypeStruct((NB * NX, HALF, QW), bf16),
        [SMEM] + [VMEM] * (NX + 2),
        flops=2 * 128 * 128 * 128 * 8,
        name="attend",
    )(lengths, own_part, *summands[1:], cosine, sine)

    out_own, attended = lax.optimization_barrier((out_own, attended))
    out_other = lax.ppermute(out_own, "core", swap)

    slab = lax.all_to_all(attended, ("two", "x"), split_axis=0, concat_axis=0, tiled=True)
    products = call(
        output_kernel,
        jax.ShapeDtypeStruct((NT * NX, HALF, BLK), bf16),
        [VMEM] * 3,
        flops=2 * 512 * 512 * 1024,
        name="output",
    )(slab, out_own, out_other)
    terms = exchange(products)

    placed, stat = call(
        layer_kernel,
        (
            jax.ShapeDtypeStruct((ROWS, FEAT), bf16),
            jax.ShapeDtypeStruct((2, BLK), f32),
        ),
        [SMEM] + [VMEM] * 5,
        flops=2 * 128 * 128 * 512,
        name="layer",
    )(
        lengths,
        terms,
        decoded,
        order,
        final_gain.reshape(1, FEAT),
        head_weight.reshape(1, FEAT),
    )
    hidden = lax.all_to_all(placed, ("x",) + Z + ("core",), split_axis=0, concat_axis=0, tiled=True)
    hidden = hidden.reshape(NX, NZ, NC * CAP, FEAT).transpose(1, 0, 2, 3).reshape(ROWS, FEAT)
    stat = lax.psum(stat[:, :RESP], TP)
    rewards = lax.rsqrt(stat[0] / D + norm_eps) * stat[1]
    return (hidden, rewards)


def solution(mesh):
    grid = Mesh(mesh.devices.reshape(NQ, NB, NQ, NB, NX, NC), TP + FSDP)
    return jax.shard_map(
        body,
        mesh=grid,
        in_specs=(
            P(FSDP, TP),
            P(FSDP, None),
            P(FSDP, None),
            P(),
            P(FSDP, TP),
            P(FSDP, None),
            P(FSDP, None),
            P(TP, FSDP),
            P(TP),
            P(TP),
        ),
        out_specs=(P(FSDP, TP), P(FSDP)),
        check_vma=False,
    )
```

```python
import jax
import jax.numpy as jnp
from jax import lax
from jax.experimental import pallas as pl
from jax.experimental.pallas import tpu as pltpu
from jax.sharding import Mesh, PartitionSpec as P

D = 4096
HD = 128
QH = 32
KVH = 2
NT, NZ, NX, NC = 8, 8, 4, 2
NQ, NB = 4, 2
TP = ("four", "two")
Z = ("quad", "pair")
FSDP = Z + ("x", "core")
ORDER = (4, 6, 3, 7, 0, 1, 5, 2)
AT = tuple(ORDER.index(t) for t in range(NT))
ROWS = 128
FEAT = D // NT
BLK = 128
QW = QH * HD // NT
PW = QW + 2 * HD
HEADS = QW // HD
HALF = ROWS // NB
EXTRA = 16
RESP = 8
CAP = 2

norm_eps = 1e-06
rope_base = 1000000.0
neg_fill = -1e30

bf16 = jnp.bfloat16
f32 = jnp.float32

VMEM = pl.BlockSpec(memory_space=pltpu.VMEM)
ANY = pl.BlockSpec(memory_space=pl.ANY)
SMEM = pl.BlockSpec(memory_space=pltpu.SMEM)


def call(kernel, out_shape, in_specs, scratch=(), flops=0, name=None, vmem=24):
    return pl.pallas_call(
        kernel,
        out_shape=out_shape,
        in_specs=in_specs,
        out_specs=jax.tree.map(lambda _: VMEM, out_shape),
        scratch_shapes=list(scratch),
        compiler_params=pltpu.CompilerParams(vmem_limit_bytes=vmem * 1024 * 1024),
        cost_estimate=pl.CostEstimate(flops=flops, bytes_accessed=4 << 20, transcendentals=0),
        name=name,
    )


def iota(shape, axis):
    return lax.broadcasted_iota(jnp.int32, shape, axis)


def eye_mask():
    return iota((ROWS, ROWS), 0) == iota((ROWS, ROWS), 1)


def resp_starts(lengths_ref, rows):
    end = jnp.int32(0)
    start = jnp.zeros_like(rows)
    for j in range(RESP):
        end = end + lengths_ref[0, j]
        start = jnp.where(rows >= end, end, start)
    return start


def prepare_kernel(
    rows, query, key, value, out_w, sent, shard, out_sent, rows_ref, query_ref, kv_ref, out_ref, sems
):
    head = pl.ds(pl.multiple_of(lax.axis_index(TP) // (NT // KVH) * HD, HD), HD)
    moves = (
        (rows, rows_ref),
        (query, query_ref),
        (key.at[:, head], kv_ref.at[0]),
        (value.at[:, head], kv_ref.at[1]),
        (out_w, out_ref),
    )
    copies = [pltpu.make_async_copy(m[0], m[1], sems.at[i]) for i, m in enumerate(moves)]
    for copy in copies:
        copy.start()
    copies[0].wait()
    for g in range(NX):
        block = rows_ref[:, g * BLK : (g + 1) * BLK]
        for t in range(NT):
            sent[t * NX + g] = block
    for copy in copies[1:]:
        copy.wait()
    shard[:, :QW] = query_ref[...]
    shard[:, QW : QW + HD] = kv_ref[0]
    shard[:, QW + HD :] = kv_ref[1]
    for i in range(NB * NZ):
        out_sent[i] = out_ref[...]


def table_kernel(lengths_ref, freq_ref, line_ref, cosine_ref, sine_ref, order_ref):
    rows = iota((ROWS, ROWS), 0)
    cols = iota((ROWS, ROWS), 1)
    angles = (rows - resp_starts(lengths_ref, rows)).astype(f32) * freq_ref[...]
    sine = jnp.sin(angles)
    cosine_ref[...] = jnp.cos(angles)
    sine_ref[...] = jnp.where(cols < HD // 2, -sine, sine)
    dest_line = line_ref[...]
    dest_column = jnp.sum(jnp.where(rows == cols, dest_line, 0), axis=1, keepdims=True)
    same = (dest_column == dest_line) & (rows < cols)
    rank = jnp.sum(same.astype(jnp.int32), axis=0, keepdims=True)
    z, x, c = dest_line // (NX * NC), dest_line // NC % NX, dest_line % NC
    place = (x * NZ + z) * NC + c
    order_ref[...] = (rows == CAP * place + rank).astype(f32).astype(bf16)


def project_kernel(
    x_ref, own_ref, other_ref, gain_ref, out0, out1, out2, out3, xs_ref, w_ref
):
    first = lax.axis_index("core") == 0
    outs = (out0, out1, out2, out3)
    for t in range(NT):
        own, other = own_ref[t], other_ref[t]
        w_ref[t * BLK : t * BLK + BLK // 2, :] = jnp.where(first, own, other)
        w_ref[t * BLK + BLK // 2 : (t + 1) * BLK, :] = jnp.where(first, other, own)
    eye = eye_mask()
    for g in range(NX):
        square = jnp.zeros((ROWS, BLK), f32)
        group = lax.rem(lax.axis_index("x") + g, NX)
        for t in range(NT):
            wide = x_ref[AT[t] * NX + group].astype(f32)
            square = square + wide * wide
            xs_ref[g * ROWS : (g + 1) * ROWS, t * BLK : (t + 1) * BLK] = (
                wide * gain_ref[t : t + 1, :].astype(f32)
            ).astype(bf16)
        total = jnp.sum(square, axis=1, keepdims=True)
        line = jnp.sum(jnp.where(eye, total, 0.0), axis=0, keepdims=True)
        high = line.astype(bf16).astype(f32)
        low = line - high
        which = iota((EXTRA, ROWS), 0)
        tail = jnp.where(which == 0, high, jnp.where(which == 1, low, 0.0)).astype(bf16)
        outs[g][PW:, :] = tail
    for n in range(PW // 256):
        cols = slice(n * 256, (n + 1) * 256)
        part = jnp.dot(xs_ref[...], w_ref[:, cols], preferred_element_type=f32)
        for g in range(NX):
            rows = part[g * ROWS : (g + 1) * ROWS].astype(bf16)
            outs[g][n * 256 : n * 256 + ROWS, :] = rows[:, :HD]
            outs[g][n * 256 + ROWS : (n + 1) * 256, :] = rows[:, HD:]


def attend_kernel(lengths_ref, part0, part1, part2, part3, cosine_ref, sine_ref, out_ref):
    parts = (part0, part1, part2, part3)
    eye = eye_mask()
    line = jnp.zeros((EXTRA, ROWS), f32)
    for i in range(NX):
        line = line + parts[i][PW:, :].astype(f32)
    line = jnp.sum(line, axis=0, keepdims=True)
    total = jnp.sum(jnp.where(eye, line, 0.0), axis=1, keepdims=True)
    scale = lax.rsqrt(total * (1.0 / D) + norm_eps)

    rows = iota((ROWS, ROWS), 0)
    cols = iota((ROWS, ROWS), 1)
    start = resp_starts(lengths_ref, rows)
    allowed = (cols >= start) & (cols <= rows)
    cosine, sine = cosine_ref[...], sine_ref[...]

    def columns(at):
        summed = parts[0][at : at + HD, :].astype(f32)
        for part in parts[1:]:
            summed = summed + part[at : at + HD, :].astype(f32)
        return summed * scale

    def rope(v):
        return (v * cosine + pltpu.roll(v, HD // 2, 1) * sine).astype(bf16)

    keys = rope(columns(QW))
    values = columns(QW + HD).astype(bf16)
    for h in range(HEADS):
        queries = rope(columns(h * HD))
        scores = lax.dot_general(
            queries, keys, (((1,), (1,)), ((), ())), preferred_element_type=f32
        ) * (HD**-0.5)
        scores = jnp.where(allowed, scores, neg_fill)
        top = jnp.max(scores, axis=1, keepdims=True)
        probs = jnp.where(allowed, jnp.exp(scores - top), 0.0)
        sums = jnp.sum(probs, axis=1, keepdims=True)
        weighted = jnp.dot(probs.astype(bf16), values, preferred_element_type=f32)
        result = (weighted / sums).astype(bf16)
        for b in range(NB):
            for g in range(NX):
                out_ref[g * NB + b, :, h * HD : (h + 1) * HD] = result[b * HALF : (b + 1) * HALF]


def output_kernel(x_ref, own_ref, other_ref, out_ref):
    first = lax.axis_index("core") == 0
    for n in range(NT // 2):
        part = None
        for b in range(NB):
            rows = []
            for z in (2 * n, 2 * n + 1):
                own, other = own_ref[z * NB + b], other_ref[z * NB + b]
                rows += [jnp.where(first, own, other), jnp.where(first, other, own)]
            x = jnp.concatenate([x_ref[g * NB + b] for g in range(NX)])
            term = lax.dot_general(
                x,
                jnp.concatenate(rows),
                (((1,), (1,)), ((), ())),
                preferred_element_type=f32,
            )
            part = term if part is None else part + term
        for g in range(NX):
            rows = part[g * HALF : (g + 1) * HALF].astype(bf16)
            out_ref[AT[2 * n] * NX + g] = rows[:, :BLK]
            out_ref[AT[2 * n + 1] * NX + g] = rows[:, BLK:]


def layer_kernel(
    lengths_ref, parts_ref, rows_ref, order_ref, final_ref, head_ref, out_ref, stat_ref
):
    square = jnp.zeros((ROWS, BLK), f32)
    product = jnp.zeros((ROWS, BLK), f32)
    for g in range(NX):
        cols = slice(g * BLK, (g + 1) * BLK)
        halves = []
        for b in range(NB):
            half = parts_ref[AT[b] * NX + g].astype(f32)
            for t in range(b + NB, NT, NB):
                half = half + parts_ref[AT[t] * NX + g].astype(f32)
            halves.append(half)
        update = jnp.concatenate(halves)
        layer = (rows_ref[:, cols].astype(f32) + update).astype(bf16)
        wide = layer.astype(f32)
        square = square + wide * wide
        product = product + wide * final_ref[:, cols].astype(f32) * head_ref[:, cols].astype(f32)
        out_ref[:, cols] = jnp.dot(order_ref[...], layer, preferred_element_type=f32).astype(bf16)

    lane = iota((1, BLK), 1)
    last = jnp.full((1, BLK), -1, jnp.int32)
    end = jnp.int32(0)
    for j in range(RESP):
        end = end + lengths_ref[0, j]
        last = jnp.where(lane == j, end - 1, last)
    pick = iota((ROWS, BLK), 0) == last
    for at, part in ((0, square), (1, product)):
        column = jnp.sum(part, axis=1, keepdims=True)
        stat_ref[at : at + 1, :] = jnp.sum(jnp.where(pick, column, 0.0), axis=0, keepdims=True)


def exchange(blocks):
    return lax.all_to_all(
        blocks,
        TP + ("x",),
        split_axis=0,
        concat_axis=0,
        tiled=True,
        axis_index_groups=[[t * NX + g for t in ORDER for g in range(NX)]],
    )


def body(
    decoded,
    lengths,
    destination,
    attn_gain,
    query_weight,
    key_weight,
    value_weight,
    out_weight,
    final_gain,
    head_weight,
):
    me_x = lax.axis_index("x")
    swap = [(0, 1), (1, 0)]

    sent, shard, out_sent = call(
        prepare_kernel,
        (
            jax.ShapeDtypeStruct((NT * NX, ROWS, BLK), bf16),
            jax.ShapeDtypeStruct((D // (NZ * NX * NC), PW), bf16),
            jax.ShapeDtypeStruct((NB * NZ, D // (NZ * NX * NC), QW), bf16),
        ),
        [ANY] * 5,
        [
            pltpu.VMEM((ROWS, FEAT), bf16),
            pltpu.VMEM((D // (NZ * NX * NC), QW), bf16),
            pltpu.VMEM((2, D // (NZ * NX * NC), HD), bf16),
            pltpu.VMEM((D // (NZ * NX * NC), QW), bf16),
            pltpu.SemaphoreType.DMA((5,)),
        ],
        name="prepare",
        vmem=60,
    )(decoded, query_weight, key_weight, value_weight, out_weight.T)
    tokens = exchange(sent)
    own = lax.all_gather(lax.all_gather(shard, "pair"), "quad")
    own = own.reshape((NZ,) + shard.shape)
    other = lax.ppermute(own, "core", swap)
    gain = lax.dynamic_slice_in_dim(attn_gain.reshape(NT, NX, BLK), me_x, 1, 1)[:, 0]

    out_sent, tokens, own = lax.optimization_barrier((out_sent, tokens, own))
    out_own = lax.all_to_all(out_sent, Z + ("two",), split_axis=0, concat_axis=0, tiled=True)

    block = jax.ShapeDtypeStruct((PW + EXTRA, HD), bf16)
    parts = call(
        project_kernel,
        (block,) * NX,
        [VMEM] * 4,
        [pltpu.VMEM((NX * ROWS, NT * BLK), bf16), pltpu.VMEM((NT * BLK, PW), bf16)],
        flops=2 * 512 * 1024 * 768,
        name="project",
    )(tokens, own, other, gain)
    summands = [parts[0]] + [
        lax.ppermute(parts[s], "x", [(i, (i + s) % NX) for i in range(NX)]) for s in (2, 3, 1)
    ]

    half = jnp.arange(HD // 2, dtype=f32)
    freq = rope_base ** (-(half * 2.0 / HD))
    freq = jnp.concatenate([freq, freq])[None]
    own_part, after, line = lax.optimization_barrier(
        (summands[0], lengths, destination.reshape(1, ROWS))
    )
    cosine, sine, order = call(
        table_kernel,
        (jax.ShapeDtypeStruct((ROWS, HD), f32),) * 2 + (jax.ShapeDtypeStruct((ROWS, ROWS), bf16),),
        [SMEM, VMEM, VMEM],
        name="tables",
    )(after, freq, line)
    attended = call(
        attend_kernel,
        jax.ShapeDtypeStruct((NB * NX, HALF, QW), bf16),
        [SMEM] + [VMEM] * (NX + 2),
        flops=2 * 128 * 128 * 128 * 8,
        name="attend",
    )(lengths, own_part, *summands[1:], cosine, sine)

    out_own, attended = lax.optimization_barrier((out_own, attended))
    out_other = lax.ppermute(out_own, "core", swap)

    slab = lax.all_to_all(attended, ("x", "two"), split_axis=0, concat_axis=0, tiled=True)
    products = call(
        output_kernel,
        jax.ShapeDtypeStruct((NT * NX, HALF, BLK), bf16),
        [VMEM] * 3,
        flops=2 * 512 * 512 * 1024,
        name="output",
    )(slab, out_own, out_other)
    terms = exchange(products)

    placed, stat = call(
        layer_kernel,
        (
            jax.ShapeDtypeStruct((ROWS, FEAT), bf16),
            jax.ShapeDtypeStruct((2, BLK), f32),
        ),
        [SMEM] + [VMEM] * 5,
        flops=2 * 128 * 128 * 512,
        name="layer",
    )(
        lengths,
        terms,
        decoded,
        order,
        final_gain.reshape(1, FEAT),
        head_weight.reshape(1, FEAT),
    )
    hidden = lax.all_to_all(placed, ("x",) + Z + ("core",), split_axis=0, concat_axis=0, tiled=True)
    hidden = hidden.reshape(NX, NZ, NC * CAP, FEAT).transpose(1, 0, 2, 3).reshape(ROWS, FEAT)
    stat = lax.psum(stat[:, :RESP], TP)
    rewards = lax.rsqrt(stat[0] / D + norm_eps) * stat[1]
    return (hidden, rewards)


def solution(mesh):
    grid = Mesh(mesh.devices.reshape(NQ, NB, NQ, NB, NX, NC), TP + FSDP)
    return jax.shard_map(
        body,
        mesh=grid,
        in_specs=(
            P(FSDP, TP),
            P(FSDP, None),
            P(FSDP, None),
            P(),
            P(FSDP, TP),
            P(FSDP, None),
            P(FSDP, None),
            P(TP, FSDP),
            P(TP),
            P(TP),
        ),
        out_specs=(P(FSDP, TP), P(FSDP)),
        check_vma=False,
    )
```

```python
import jax
import jax.numpy as jnp
from jax import lax
from jax.experimental import pallas as pl
from jax.experimental.pallas import tpu as pltpu
from jax.sharding import Mesh, PartitionSpec as P

D = 4096
HD = 128
QH = 32
KVH = 2
NT, NZ, NX, NC = 8, 8, 4, 2
NQ, NB = 4, 2
TP = ("four", "two")
Z = ("quad", "pair")
FSDP = Z + ("x", "core")
ORDER = (4, 6, 3, 7, 0, 1, 5, 2)
AT = tuple(ORDER.index(t) for t in range(NT))
ROWS = 128
FEAT = D // NT
BLK = 128
QW = QH * HD // NT
PW = QW + 2 * HD
HEADS = QW // HD
HALF = ROWS // NB
EXTRA = 16
RESP = 8
CAP = 2

norm_eps = 1e-06
rope_base = 1000000.0
neg_fill = -1e30

bf16 = jnp.bfloat16
f32 = jnp.float32

VMEM = pl.BlockSpec(memory_space=pltpu.VMEM)
ANY = pl.BlockSpec(memory_space=pl.ANY)
SMEM = pl.BlockSpec(memory_space=pltpu.SMEM)


def call(kernel, out_shape, in_specs, scratch=(), flops=0, name=None, vmem=24):
    return pl.pallas_call(
        kernel,
        out_shape=out_shape,
        in_specs=in_specs,
        out_specs=jax.tree.map(lambda _: VMEM, out_shape),
        scratch_shapes=list(scratch),
        compiler_params=pltpu.CompilerParams(vmem_limit_bytes=vmem * 1024 * 1024),
        cost_estimate=pl.CostEstimate(flops=flops, bytes_accessed=4 << 20, transcendentals=0),
        name=name,
    )


def iota(shape, axis):
    return lax.broadcasted_iota(jnp.int32, shape, axis)


def eye_mask():
    return iota((ROWS, ROWS), 0) == iota((ROWS, ROWS), 1)


def resp_starts(lengths_ref, rows):
    end = jnp.int32(0)
    start = jnp.zeros_like(rows)
    for j in range(RESP):
        end = end + lengths_ref[0, j]
        start = jnp.where(rows >= end, end, start)
    return start


def prepare_kernel(
    rows, query, key, value, out_w, sent, shard, out_sent, rows_ref, query_ref, kv_ref, out_ref, sems
):
    head = pl.ds(pl.multiple_of(lax.axis_index(TP) // (NT // KVH) * HD, HD), HD)
    moves = (
        (rows, rows_ref),
        (query, query_ref),
        (key.at[:, head], kv_ref.at[0]),
        (value.at[:, head], kv_ref.at[1]),
        (out_w, out_ref),
    )
    copies = [pltpu.make_async_copy(m[0], m[1], sems.at[i]) for i, m in enumerate(moves)]
    for copy in copies:
        copy.start()
    copies[0].wait()
    for g in range(NX):
        block = rows_ref[:, g * BLK : (g + 1) * BLK]
        for t in range(NT):
            sent[t * NX + g] = block
    for copy in copies[1:]:
        copy.wait()
    shard[:, :QW] = query_ref[...]
    shard[:, QW : QW + HD] = kv_ref[0]
    shard[:, QW + HD :] = kv_ref[1]
    for i in range(NB * NZ):
        out_sent[i] = out_ref[...]


def table_kernel(lengths_ref, freq_ref, line_ref, cosine_ref, sine_ref, order_ref):
    rows = iota((ROWS, ROWS), 0)
    cols = iota((ROWS, ROWS), 1)
    angles = (rows - resp_starts(lengths_ref, rows)).astype(f32) * freq_ref[...]
    sine = jnp.sin(angles)
    cosine_ref[...] = jnp.cos(angles)
    sine_ref[...] = jnp.where(cols < HD // 2, -sine, sine)
    dest_line = line_ref[...]
    dest_column = jnp.sum(jnp.where(rows == cols, dest_line, 0), axis=1, keepdims=True)
    same = (dest_column == dest_line) & (rows < cols)
    rank = jnp.sum(same.astype(jnp.int32), axis=0, keepdims=True)
    z, x, c = dest_line // (NX * NC), dest_line // NC % NX, dest_line % NC
    place = (x * NZ + z) * NC + c
    order_ref[...] = (rows == CAP * place + rank).astype(f32).astype(bf16)


def project_kernel(
    x_ref, own_ref, other_ref, gain_ref, out0, out1, out2, out3, xs_ref
):
    first = lax.axis_index("core") == 0
    outs = (out0, out1, out2, out3)
    left = iota((ROWS, BLK), 1) < BLK // 2
    eye = eye_mask()
    for g in range(NX):
        square = jnp.zeros((ROWS, BLK), f32)
        group = lax.rem(lax.axis_index("x") + g, NX)
        for t in range(0, NT, 2):
            pair = []
            for u in (t, t + 1):
                wide = x_ref[AT[u] * NX + group].astype(f32)
                square = square + wide * wide
                pair.append(wide * gain_ref[u : u + 1, :].astype(f32))
            zero = jnp.where(left, pair[0], pltpu.roll(pair[1], BLK // 2, 1))
            one = jnp.where(left, pltpu.roll(pair[0], BLK // 2, 1), pair[1])
            rows, at = slice(g * ROWS, (g + 1) * ROWS), t * BLK // 2
            half = NT * BLK // 2
            xs_ref[rows, at : at + BLK] = jnp.where(first, zero, one).astype(bf16)
            xs_ref[rows, half + at : half + at + BLK] = jnp.where(first, one, zero).astype(bf16)
        total = jnp.sum(square, axis=1, keepdims=True)
        line = jnp.sum(jnp.where(eye, total, 0.0), axis=0, keepdims=True)
        high = line.astype(bf16).astype(f32)
        low = line - high
        which = iota((EXTRA, ROWS), 0)
        tail = jnp.where(which == 0, high, jnp.where(which == 1, low, 0.0)).astype(bf16)
        outs[g][PW:, :] = tail
    for n in range(PW // 256):
        cols = slice(n * 256, (n + 1) * 256)
        half = NT * BLK // 2
        part = jnp.dot(
            xs_ref[:, :half], own_ref[:, :, cols].reshape(half, 256), preferred_element_type=f32
        ) + jnp.dot(
            xs_ref[:, half:], other_ref[:, :, cols].reshape(half, 256), preferred_element_type=f32
        )
        for g in range(NX):
            rows = part[g * ROWS : (g + 1) * ROWS].astype(bf16)
            outs[g][n * 256 : n * 256 + ROWS, :] = rows[:, :HD]
            outs[g][n * 256 + ROWS : (n + 1) * 256, :] = rows[:, HD:]


def attend_kernel(lengths_ref, part0, part1, part2, part3, cosine_ref, sine_ref, out_ref):
    parts = (part0, part1, part2, part3)
    eye = eye_mask()
    line = jnp.zeros((EXTRA, ROWS), f32)
    for i in range(NX):
        line = line + parts[i][PW:, :].astype(f32)
    line = jnp.sum(line, axis=0, keepdims=True)
    total = jnp.sum(jnp.where(eye, line, 0.0), axis=1, keepdims=True)
    scale = lax.rsqrt(total * (1.0 / D) + norm_eps)

    rows = iota((ROWS, ROWS), 0)
    cols = iota((ROWS, ROWS), 1)
    start = resp_starts(lengths_ref, rows)
    allowed = (cols >= start) & (cols <= rows)
    cosine, sine = cosine_ref[...], sine_ref[...]

    def columns(at):
        summed = parts[0][at : at + HD, :].astype(f32)
        for part in parts[1:]:
            summed = summed + part[at : at + HD, :].astype(f32)
        return summed * scale

    def rope(v):
        return (v * cosine + pltpu.roll(v, HD // 2, 1) * sine).astype(bf16)

    keys = rope(columns(QW))
    values = columns(QW + HD).astype(bf16)
    for h in range(HEADS):
        queries = rope(columns(h * HD))
        scores = lax.dot_general(
            queries, keys, (((1,), (1,)), ((), ())), preferred_element_type=f32
        ) * (HD**-0.5)
        scores = jnp.where(allowed, scores, neg_fill)
        top = jnp.max(scores, axis=1, keepdims=True)
        probs = jnp.where(allowed, jnp.exp(scores - top), 0.0)
        sums = jnp.sum(probs, axis=1, keepdims=True)
        weighted = jnp.dot(probs.astype(bf16), values, preferred_element_type=f32)
        result = (weighted / sums).astype(bf16)
        for b in range(NB):
            for g in range(NX):
                out_ref[g * NB + b, :, h * HD : (h + 1) * HD] = result[b * HALF : (b + 1) * HALF]


def output_kernel(x_ref, own_ref, other_ref, out_ref):
    first = lax.axis_index("core") == 0
    for n in range(NT // 2):
        part = None
        for b in range(NB):
            rows = []
            for z in (2 * n, 2 * n + 1):
                own, other = own_ref[z * NB + b], other_ref[z * NB + b]
                rows += [jnp.where(first, own, other), jnp.where(first, other, own)]
            x = jnp.concatenate([x_ref[g * NB + b] for g in range(NX)])
            term = lax.dot_general(
                x,
                jnp.concatenate(rows),
                (((1,), (1,)), ((), ())),
                preferred_element_type=f32,
            )
            part = term if part is None else part + term
        for g in range(NX):
            rows = part[g * HALF : (g + 1) * HALF].astype(bf16)
            out_ref[AT[2 * n] * NX + g] = rows[:, :BLK]
            out_ref[AT[2 * n + 1] * NX + g] = rows[:, BLK:]


def layer_kernel(
    lengths_ref, parts_ref, rows_ref, order_ref, final_ref, head_ref, out_ref, stat_ref
):
    square = jnp.zeros((ROWS, BLK), f32)
    product = jnp.zeros((ROWS, BLK), f32)
    for g in range(NX):
        cols = slice(g * BLK, (g + 1) * BLK)
        halves = []
        for b in range(NB):
            half = parts_ref[AT[b] * NX + g].astype(f32)
            for t in range(b + NB, NT, NB):
                half = half + parts_ref[AT[t] * NX + g].astype(f32)
            halves.append(half)
        update = jnp.concatenate(halves)
        layer = (rows_ref[:, cols].astype(f32) + update).astype(bf16)
        wide = layer.astype(f32)
        square = square + wide * wide
        product = product + wide * final_ref[:, cols].astype(f32) * head_ref[:, cols].astype(f32)
        out_ref[:, cols] = jnp.dot(order_ref[...], layer, preferred_element_type=f32).astype(bf16)

    lane = iota((1, BLK), 1)
    last = jnp.full((1, BLK), -1, jnp.int32)
    end = jnp.int32(0)
    for j in range(RESP):
        end = end + lengths_ref[0, j]
        last = jnp.where(lane == j, end - 1, last)
    pick = iota((ROWS, BLK), 0) == last
    for at, part in ((0, square), (1, product)):
        column = jnp.sum(part, axis=1, keepdims=True)
        stat_ref[at : at + 1, :] = jnp.sum(jnp.where(pick, column, 0.0), axis=0, keepdims=True)


def exchange(blocks):
    return lax.all_to_all(
        blocks,
        TP + ("x",),
        split_axis=0,
        concat_axis=0,
        tiled=True,
        axis_index_groups=[[t * NX + g for t in ORDER for g in range(NX)]],
    )


def body(
    decoded,
    lengths,
    destination,
    attn_gain,
    query_weight,
    key_weight,
    value_weight,
    out_weight,
    final_gain,
    head_weight,
):
    me_x = lax.axis_index("x")
    swap = [(0, 1), (1, 0)]

    sent, shard, out_sent = call(
        prepare_kernel,
        (
            jax.ShapeDtypeStruct((NT * NX, ROWS, BLK), bf16),
            jax.ShapeDtypeStruct((D // (NZ * NX * NC), PW), bf16),
            jax.ShapeDtypeStruct((NB * NZ, D // (NZ * NX * NC), QW), bf16),
        ),
        [ANY] * 5,
        [
            pltpu.VMEM((ROWS, FEAT), bf16),
            pltpu.VMEM((D // (NZ * NX * NC), QW), bf16),
            pltpu.VMEM((2, D // (NZ * NX * NC), HD), bf16),
            pltpu.VMEM((D // (NZ * NX * NC), QW), bf16),
            pltpu.SemaphoreType.DMA((5,)),
        ],
        name="prepare",
        vmem=60,
    )(decoded, query_weight, key_weight, value_weight, out_weight.T)
    tokens = exchange(sent)
    own = lax.all_gather(lax.all_gather(shard, "pair"), "quad")
    own = own.reshape((NZ,) + shard.shape)
    other = lax.ppermute(own, "core", swap)
    gain = lax.dynamic_slice_in_dim(attn_gain.reshape(NT, NX, BLK), me_x, 1, 1)[:, 0]

    out_sent, tokens, own = lax.optimization_barrier((out_sent, tokens, own))
    out_own = lax.all_to_all(out_sent, Z + ("two",), split_axis=0, concat_axis=0, tiled=True)

    block = jax.ShapeDtypeStruct((PW + EXTRA, HD), bf16)
    parts = call(
        project_kernel,
        (block,) * NX,
        [VMEM] * 4,
        [pltpu.VMEM((NX * ROWS, NT * BLK), bf16)],
        flops=2 * 512 * 1024 * 768,
        name="project",
    )(tokens, own, other, gain)
    summands = [parts[0]] + [
        lax.ppermute(parts[s], "x", [(i, (i + s) % NX) for i in range(NX)]) for s in (2, 3, 1)
    ]

    half = jnp.arange(HD // 2, dtype=f32)
    freq = rope_base ** (-(half * 2.0 / HD))
    freq = jnp.concatenate([freq, freq])[None]
    own_part, after, line = lax.optimization_barrier(
        (summands[0], lengths, destination.reshape(1, ROWS))
    )
    cosine, sine, order = call(
        table_kernel,
        (jax.ShapeDtypeStruct((ROWS, HD), f32),) * 2 + (jax.ShapeDtypeStruct((ROWS, ROWS), bf16),),
        [SMEM, VMEM, VMEM],
        name="tables",
    )(after, freq, line)
    attended = call(
        attend_kernel,
        jax.ShapeDtypeStruct((NB * NX, HALF, QW), bf16),
        [SMEM] + [VMEM] * (NX + 2),
        flops=2 * 128 * 128 * 128 * 8,
        name="attend",
    )(lengths, own_part, *summands[1:], cosine, sine)

    out_own, attended = lax.optimization_barrier((out_own, attended))
    out_other = lax.ppermute(out_own, "core", swap)

    slab = lax.all_to_all(attended, ("x", "two"), split_axis=0, concat_axis=0, tiled=True)
    products = call(
        output_kernel,
        jax.ShapeDtypeStruct((NT * NX, HALF, BLK), bf16),
        [VMEM] * 3,
        flops=2 * 512 * 512 * 1024,
        name="output",
    )(slab, out_own, out_other)
    terms = exchange(products)

    placed, stat = call(
        layer_kernel,
        (
            jax.ShapeDtypeStruct((ROWS, FEAT), bf16),
            jax.ShapeDtypeStruct((2, BLK), f32),
        ),
        [SMEM] + [VMEM] * 5,
        flops=2 * 128 * 128 * 512,
        name="layer",
    )(
        lengths,
        terms,
        decoded,
        order,
        final_gain.reshape(1, FEAT),
        head_weight.reshape(1, FEAT),
    )
    hidden = lax.all_to_all(placed, ("x",) + Z + ("core",), split_axis=0, concat_axis=0, tiled=True)
    hidden = hidden.reshape(NX, NZ, NC * CAP, FEAT).transpose(1, 0, 2, 3).reshape(ROWS, FEAT)
    stat = lax.psum(stat[:, :RESP], TP)
    rewards = lax.rsqrt(stat[0] / D + norm_eps) * stat[1]
    return (hidden, rewards)


def solution(mesh):
    grid = Mesh(mesh.devices.reshape(NQ, NB, NQ, NB, NX, NC), TP + FSDP)
    return jax.shard_map(
        body,
        mesh=grid,
        in_specs=(
            P(FSDP, TP),
            P(FSDP, None),
            P(FSDP, None),
            P(),
            P(FSDP, TP),
            P(FSDP, None),
            P(FSDP, None),
            P(TP, FSDP),
            P(TP),
            P(TP),
        ),
        out_specs=(P(FSDP, TP), P(FSDP)),
        check_vma=False,
    )
```

```python
import jax
import jax.numpy as jnp
from jax import lax
from jax.experimental import pallas as pl
from jax.experimental.pallas import tpu as pltpu
from jax.sharding import Mesh, PartitionSpec as P

D = 4096
HD = 128
QH = 32
KVH = 2
NT, NZ, NX, NC = 8, 8, 4, 2
NQ, NB = 4, 2
TP = ("four", "two")
Z = ("quad", "pair")
FSDP = Z + ("x", "core")
ORDER = (4, 6, 3, 7, 0, 1, 5, 2)
AT = tuple(ORDER.index(t) for t in range(NT))
ROWS = 128
FEAT = D // NT
BLK = 128
QW = QH * HD // NT
PW = QW + 2 * HD
HEADS = QW // HD
HALF = ROWS // NB
EXTRA = 16
RESP = 8
CAP = 2

norm_eps = 1e-06
rope_base = 1000000.0
neg_fill = -1e30

bf16 = jnp.bfloat16
f32 = jnp.float32

VMEM = pl.BlockSpec(memory_space=pltpu.VMEM)
ANY = pl.BlockSpec(memory_space=pl.ANY)
SMEM = pl.BlockSpec(memory_space=pltpu.SMEM)


def call(kernel, out_shape, in_specs, scratch=(), flops=0, name=None, vmem=24):
    return pl.pallas_call(
        kernel,
        out_shape=out_shape,
        in_specs=in_specs,
        out_specs=jax.tree.map(lambda _: VMEM, out_shape),
        scratch_shapes=list(scratch),
        compiler_params=pltpu.CompilerParams(vmem_limit_bytes=vmem * 1024 * 1024),
        cost_estimate=pl.CostEstimate(flops=flops, bytes_accessed=4 << 20, transcendentals=0),
        name=name,
    )


def iota(shape, axis):
    return lax.broadcasted_iota(jnp.int32, shape, axis)


def eye_mask():
    return iota((ROWS, ROWS), 0) == iota((ROWS, ROWS), 1)


def resp_starts(lengths_ref, rows):
    end = jnp.int32(0)
    start = jnp.zeros_like(rows)
    for j in range(RESP):
        end = end + lengths_ref[0, j]
        start = jnp.where(rows >= end, end, start)
    return start


def prepare_kernel(
    rows, query, key, value, out_w, sent, shard, out_sent, rows_ref, query_ref, kv_ref, out_ref, sems
):
    head = pl.ds(pl.multiple_of(lax.axis_index(TP) // (NT // KVH) * HD, HD), HD)
    moves = (
        (rows, rows_ref),
        (query, query_ref),
        (key.at[:, head], kv_ref.at[0]),
        (value.at[:, head], kv_ref.at[1]),
        (out_w, out_ref),
    )
    copies = [pltpu.make_async_copy(m[0], m[1], sems.at[i]) for i, m in enumerate(moves)]
    for copy in copies:
        copy.start()
    copies[0].wait()
    for g in range(NX):
        block = rows_ref[:, g * BLK : (g + 1) * BLK]
        for t in range(NT):
            sent[t * NX + g] = block
    for copy in copies[1:]:
        copy.wait()
    shard[:, :QW] = query_ref[...]
    shard[:, QW : QW + HD] = kv_ref[0]
    shard[:, QW + HD :] = kv_ref[1]
    for i in range(NB * NZ):
        out_sent[i] = out_ref[...]


def table_kernel(lengths_ref, freq_ref, line_ref, cosine_ref, sine_ref, order_ref):
    rows = iota((ROWS, ROWS), 0)
    cols = iota((ROWS, ROWS), 1)
    angles = (rows - resp_starts(lengths_ref, rows)).astype(f32) * freq_ref[...]
    sine = jnp.sin(angles)
    cosine_ref[...] = jnp.cos(angles)
    sine_ref[...] = jnp.where(cols < HD // 2, -sine, sine)
    dest_line = line_ref[...]
    dest_column = jnp.sum(jnp.where(rows == cols, dest_line, 0), axis=1, keepdims=True)
    same = (dest_column == dest_line) & (rows < cols)
    rank = jnp.sum(same.astype(jnp.int32), axis=0, keepdims=True)
    z, x, c = dest_line // (NX * NC), dest_line // NC % NX, dest_line % NC
    place = (x * NZ + z) * NC + c
    order_ref[...] = (rows == CAP * place + rank).astype(f32).astype(bf16)


def project_kernel(
    x_ref, own_ref, other_ref, gain_ref, out0, out1, out2, out3, xs_ref, w_ref
):
    first = lax.axis_index("core") == 0
    outs = (out0, out1, out2, out3)
    for t in range(NT):
        own, other = own_ref[t], other_ref[t]
        w_ref[t * BLK : t * BLK + BLK // 2, :] = jnp.where(first, own, other)
        w_ref[t * BLK + BLK // 2 : (t + 1) * BLK, :] = jnp.where(first, other, own)
    eye = eye_mask()
    for g in range(NX):
        square = jnp.zeros((ROWS, BLK), f32)
        group = lax.rem(lax.axis_index("x") + g, NX)
        for t in range(NT):
            wide = x_ref[AT[t] * NX + group].astype(f32)
            square = square + wide * wide
            xs_ref[g * ROWS : (g + 1) * ROWS, t * BLK : (t + 1) * BLK] = (
                wide * gain_ref[t : t + 1, :].astype(f32)
            ).astype(bf16)
        total = jnp.sum(square, axis=1, keepdims=True)
        line = jnp.sum(jnp.where(eye, total, 0.0), axis=0, keepdims=True)
        high = line.astype(bf16).astype(f32)
        low = line - high
        which = iota((EXTRA, ROWS), 0)
        tail = jnp.where(which == 0, high, jnp.where(which == 1, low, 0.0)).astype(bf16)
        outs[g][PW:, :] = tail
    for n in range(PW // 256):
        cols = slice(n * 256, (n + 1) * 256)
        part = jnp.dot(xs_ref[...], w_ref[:, cols], preferred_element_type=f32)
        for g in range(NX):
            rows = part[g * ROWS : (g + 1) * ROWS].astype(bf16)
            outs[g][n * 256 : n * 256 + ROWS, :] = rows[:, :HD]
            outs[g][n * 256 + ROWS : (n + 1) * 256, :] = rows[:, HD:]


def attend_kernel(lengths_ref, part0, part1, part2, part3, cosine_ref, sine_ref, out_ref):
    parts = (part0, part1, part2, part3)
    eye = eye_mask()
    line = jnp.zeros((EXTRA, ROWS), f32)
    for i in range(NX):
        line = line + parts[i][PW:, :].astype(f32)
    line = jnp.sum(line, axis=0, keepdims=True)
    total = jnp.sum(jnp.where(eye, line, 0.0), axis=1, keepdims=True)
    scale = lax.rsqrt(total * (1.0 / D) + norm_eps)

    rows = iota((ROWS, ROWS), 0)
    cols = iota((ROWS, ROWS), 1)
    start = resp_starts(lengths_ref, rows)
    allowed = (cols >= start) & (cols <= rows)
    cosine, sine = cosine_ref[...], sine_ref[...]

    def columns(at):
        summed = parts[0][at : at + HD, :].astype(f32)
        for part in parts[1:]:
            summed = summed + part[at : at + HD, :].astype(f32)
        return summed * scale

    def rope(v):
        return (v * cosine + pltpu.roll(v, HD // 2, 1) * sine).astype(bf16)

    keys = rope(columns(QW))
    values = columns(QW + HD).astype(bf16)
    for h in range(HEADS):
        queries = rope(columns(h * HD))
        scores = lax.dot_general(
            queries, keys, (((1,), (1,)), ((), ())), preferred_element_type=f32
        ) * (HD**-0.5)
        scores = jnp.where(allowed, scores, neg_fill)
        top = jnp.max(scores, axis=1, keepdims=True)
        probs = jnp.where(allowed, jnp.exp(scores - top), 0.0)
        sums = jnp.sum(probs, axis=1, keepdims=True)
        weighted = jnp.dot(probs.astype(bf16), values, preferred_element_type=f32)
        result = (weighted / sums).astype(bf16)
        for b in range(NB):
            for g in range(NX):
                out_ref[b * NX + g, :, h * HD : (h + 1) * HD] = result[b * HALF : (b + 1) * HALF]


def output_kernel(x_ref, own_ref, other_ref, out_ref):
    first = lax.axis_index("core") == 0
    for n in range(NT // 2):
        part = None
        for b in range(NB):
            rows = []
            for z in (2 * n, 2 * n + 1):
                own, other = own_ref[z * NB + b], other_ref[z * NB + b]
                rows += [jnp.where(first, own, other), jnp.where(first, other, own)]
            x = x_ref[b * NX : (b + 1) * NX].reshape(NX * HALF, QW)
            term = lax.dot_general(
                x,
                jnp.concatenate(rows),
                (((1,), (1,)), ((), ())),
                preferred_element_type=f32,
            )
            part = term if part is None else part + term
        for g in range(NX):
            rows = part[g * HALF : (g + 1) * HALF].astype(bf16)
            out_ref[AT[2 * n] * NX + g] = rows[:, :BLK]
            out_ref[AT[2 * n + 1] * NX + g] = rows[:, BLK:]


def layer_kernel(
    lengths_ref, parts_ref, rows_ref, order_ref, final_ref, head_ref, out_ref, stat_ref
):
    square = jnp.zeros((ROWS, BLK), f32)
    product = jnp.zeros((ROWS, BLK), f32)
    for g in range(NX):
        cols = slice(g * BLK, (g + 1) * BLK)
        halves = []
        for b in range(NB):
            half = parts_ref[AT[b] * NX + g].astype(f32)
            for t in range(b + NB, NT, NB):
                half = half + parts_ref[AT[t] * NX + g].astype(f32)
            halves.append(half)
        update = jnp.concatenate(halves)
        layer = (rows_ref[:, cols].astype(f32) + update).astype(bf16)
        wide = layer.astype(f32)
        square = square + wide * wide
        product = product + wide * final_ref[:, cols].astype(f32) * head_ref[:, cols].astype(f32)
        out_ref[:, cols] = jnp.dot(order_ref[...], layer, preferred_element_type=f32).astype(bf16)

    lane = iota((1, BLK), 1)
    last = jnp.full((1, BLK), -1, jnp.int32)
    end = jnp.int32(0)
    for j in range(RESP):
        end = end + lengths_ref[0, j]
        last = jnp.where(lane == j, end - 1, last)
    pick = iota((ROWS, BLK), 0) == last
    for at, part in ((0, square), (1, product)):
        column = jnp.sum(part, axis=1, keepdims=True)
        stat_ref[at : at + 1, :] = jnp.sum(jnp.where(pick, column, 0.0), axis=0, keepdims=True)


def exchange(blocks):
    return lax.all_to_all(
        blocks,
        TP + ("x",),
        split_axis=0,
        concat_axis=0,
        tiled=True,
        axis_index_groups=[[t * NX + g for t in ORDER for g in range(NX)]],
    )


def body(
    decoded,
    lengths,
    destination,
    attn_gain,
    query_weight,
    key_weight,
    value_weight,
    out_weight,
    final_gain,
    head_weight,
):
    me_x = lax.axis_index("x")
    swap = [(0, 1), (1, 0)]

    sent, shard, out_sent = call(
        prepare_kernel,
        (
            jax.ShapeDtypeStruct((NT * NX, ROWS, BLK), bf16),
            jax.ShapeDtypeStruct((D // (NZ * NX * NC), PW), bf16),
            jax.ShapeDtypeStruct((NB * NZ, D // (NZ * NX * NC), QW), bf16),
        ),
        [ANY] * 5,
        [
            pltpu.VMEM((ROWS, FEAT), bf16),
            pltpu.VMEM((D // (NZ * NX * NC), QW), bf16),
            pltpu.VMEM((2, D // (NZ * NX * NC), HD), bf16),
            pltpu.VMEM((D // (NZ * NX * NC), QW), bf16),
            pltpu.SemaphoreType.DMA((5,)),
        ],
        name="prepare",
        vmem=60,
    )(decoded, query_weight, key_weight, value_weight, out_weight.T)
    tokens = exchange(sent)
    own = lax.all_gather(lax.all_gather(shard, "pair"), "quad")
    own = own.reshape((NZ,) + shard.shape)
    other = lax.ppermute(own, "core", swap)
    gain = lax.dynamic_slice_in_dim(attn_gain.reshape(NT, NX, BLK), me_x, 1, 1)[:, 0]

    out_sent, tokens, own = lax.optimization_barrier((out_sent, tokens, own))
    out_own = lax.all_to_all(out_sent, Z + ("two",), split_axis=0, concat_axis=0, tiled=True)

    block = jax.ShapeDtypeStruct((PW + EXTRA, HD), bf16)
    parts = call(
        project_kernel,
        (block,) * NX,
        [VMEM] * 4,
        [pltpu.VMEM((NX * ROWS, NT * BLK), bf16), pltpu.VMEM((NT * BLK, PW), bf16)],
        flops=2 * 512 * 1024 * 768,
        name="project",
    )(tokens, own, other, gain)
    summands = [parts[0]] + [
        lax.ppermute(parts[s], "x", [(i, (i + s) % NX) for i in range(NX)]) for s in (2, 3, 1)
    ]

    half = jnp.arange(HD // 2, dtype=f32)
    freq = rope_base ** (-(half * 2.0 / HD))
    freq = jnp.concatenate([freq, freq])[None]
    own_part, after, line = lax.optimization_barrier(
        (summands[0], lengths, destination.reshape(1, ROWS))
    )
    cosine, sine, order = call(
        table_kernel,
        (jax.ShapeDtypeStruct((ROWS, HD), f32),) * 2 + (jax.ShapeDtypeStruct((ROWS, ROWS), bf16),),
        [SMEM, VMEM, VMEM],
        name="tables",
    )(after, freq, line)
    attended = call(
        attend_kernel,
        jax.ShapeDtypeStruct((NB * NX, HALF, QW), bf16),
        [SMEM] + [VMEM] * (NX + 2),
        flops=2 * 128 * 128 * 128 * 8,
        name="attend",
    )(lengths, own_part, *summands[1:], cosine, sine)

    out_own, attended = lax.optimization_barrier((out_own, attended))
    out_other = lax.ppermute(out_own, "core", swap)

    slab = lax.all_to_all(attended, ("two", "x"), split_axis=0, concat_axis=0, tiled=True)
    products = call(
        output_kernel,
        jax.ShapeDtypeStruct((NT * NX, HALF, BLK), bf16),
        [VMEM] * 3,
        flops=2 * 512 * 512 * 1024,
        name="output",
    )(slab, out_own, out_other)
    terms = exchange(products)

    placed, stat = call(
        layer_kernel,
        (
            jax.ShapeDtypeStruct((ROWS, FEAT), bf16),
            jax.ShapeDtypeStruct((2, BLK), f32),
        ),
        [SMEM] + [VMEM] * 5,
        flops=2 * 128 * 128 * 512,
        name="layer",
    )(
        lengths,
        terms,
        decoded,
        order,
        final_gain.reshape(1, FEAT),
        head_weight.reshape(1, FEAT),
    )
    hidden = lax.all_to_all(placed, ("x",) + Z + ("core",), split_axis=0, concat_axis=0, tiled=True)
    hidden = hidden.reshape(NX, NZ, NC * CAP, FEAT).transpose(1, 0, 2, 3).reshape(ROWS, FEAT)
    stat = lax.psum(stat[:, :RESP], TP)
    rewards = lax.rsqrt(stat[0] / D + norm_eps) * stat[1]
    return (hidden, rewards)


def solution(mesh):
    grid = Mesh(mesh.devices.reshape(NQ, NB, NQ, NB, NX, NC), TP + FSDP)
    return jax.shard_map(
        body,
        mesh=grid,
        in_specs=(
            P(FSDP, TP),
            P(FSDP, None),
            P(FSDP, None),
            P(),
            P(FSDP, TP),
            P(FSDP, None),
            P(FSDP, None),
            P(TP, FSDP),
            P(TP),
            P(TP),
        ),
        out_specs=(P(FSDP, TP), P(FSDP)),
        check_vma=False,
    )
```
